32 devices in a mesh: grp: 2 (over y), snap: 4 (over z), clus: 4 (over x, core).
Axes of the slice: x: 2, y: 2, z: 4, core: 2. Of those that a mesh axis runs over, the one named last changes fastest.
Arguments:
- features: bfloat16 [16, 8192, 256], P(('grp', 'snap'), 'clus'), parts along dimension 0, may hold values from -6 to 6
- adj_tiles: bfloat16 [16, 64, 4, 128, 128], P(('grp', 'snap'), 'clus'), parts along dimension 0, may hold values from -0.25 to 0.25
- neighbors: int32 [16, 64, 4], P(('grp', 'snap')), parts along dimension 0, may hold values from 0 to 63, as said below
- w_struct: bfloat16 [256, 256], replicated, may hold values from -0.375 to 0.375
- pos_embed: bfloat16 [8, 256], replicated, may hold values from -3 to 3
- w_query: bfloat16 [256, 256], replicated, may hold values from -9 to 9
- w_key: bfloat16 [256, 256], replicated, may hold values from -9 to 9
- w_value: bfloat16 [256, 256], replicated, may hold values from -0.375 to 0.375
- w_out: bfloat16 [256, 256], replicated, may hold values from -0.375 to 0.375
- w_up: bfloat16 [256, 1024], replicated, may hold values from -0.375 to 0.375
- up_bias: float32 [1024], replicated, may hold values from -3 to 3
- w_down: bfloat16 [1024, 256], replicated, may hold values from -0.1875 to 0.1875
Outputs:
- layer_out: bfloat16 [16, 8192, 256], P(('grp', 'snap'), 'clus'), parts along dimension 0
The draws below stay inside these ranges and needn't reach their ends.
There are 2 independent parts, one for each index of `grp`. The reference program is written for one: setup_inputs(seed, part) draws one part's arguments, and reference() takes and returns one part's arrays. A program takes and returns all parts, laid end to end along the dimension named above; an argument that names none is the same for every part. Nothing has to cross between parts.
Inputs may be any that keep to these rules, and one draw needn't show every extreme that they name: `neighbors`: cluster c holds blocks c * 16 to (c + 1) * 16 - 1. Entry 0 of each block row names the row itself; the other entries name blocks of the row's own cluster, except that the last entry may name a block of another cluster. In each snapshot the rows of one cluster name exactly 4 distinct blocks of each other cluster.
All inputs are finite; a program needn't handle non-finite values.
Results may differ from the reference program's by a relative error of at most 0.0073.
Values may be sent and summed in bfloat16 or wider, within the bound.
No kernel may reach another device: no remote copies, remote signals or barrier semaphores. Data moves between devices by JAX's collectives and lax.ppermute only.
A program may use at most 128 MiB of HBM per device.

```python
import math
import jax
import jax.numpy as jnp
from jax import lax

D = 256
HEADS = 8
HEAD_DIM = 32
FF = 1024
BLK = 128
NBR_K = 4
BLK_CL = 16
SNAPS = 8
BLOCKS = 64
VERTS = 8192
REMOTE_MAX = 4
N_CLUS = 4


def draw_neighbors(key, part):
    first_key, second_key, third_key = jax.random.split(jax.random.fold_in(key, 4409), 3)
    rows = jnp.arange(BLOCKS, dtype=jnp.int32)
    cluster = rows // BLK_CL
    within = rows % BLK_CL
    local_pick = jax.random.randint(first_key, (SNAPS, BLOCKS, NBR_K), 0, BLK_CL, dtype=jnp.int32) + (cluster * BLK_CL)[None, :, None]
    rotate = jax.random.randint(second_key, (SNAPS, 1), 0, N_CLUS - 1, dtype=jnp.int32)
    offset = 1 + (within[None, :] // REMOTE_MAX + rotate) % (N_CLUS - 1)
    remote_local = within[None, :] % REMOTE_MAX + REMOTE_MAX * jax.random.randint(third_key, (SNAPS, BLOCKS), 0, BLK_CL // REMOTE_MAX, dtype=jnp.int32)
    remote_global = (cluster[None, :] + offset) % N_CLUS * BLK_CL + remote_local
    has_remote = within[None, :] < REMOTE_MAX * (N_CLUS - 1)
    last_slot = jnp.where(has_remote, remote_global, local_pick[:, :, NBR_K - 1])
    self_slot = jnp.broadcast_to(rows[None, :], (SNAPS, BLOCKS))
    return jnp.concatenate([self_slot[:, :, None], local_pick[:, :, 1:NBR_K - 1], last_slot[:, :, None]], axis=2).astype(jnp.int32)


def query_key_pair(key):
    shared = jax.random.fold_in(key, 7301)
    first_key, second_key = jax.random.split(shared, 2)
    scale_in = 1.0 / math.sqrt(D)
    w_first = jnp.clip(jax.random.normal(first_key, (D, D), jnp.float32), -4.0, 4.0) * scale_in
    noise = jnp.clip(jax.random.normal(second_key, (D, D), jnp.float32), -4.0, 4.0) * scale_in
    w_second = noise
    return (w_first, w_second)


def draw_w_query(key, part):
    return query_key_pair(key)[0].astype(jnp.bfloat16)


def draw_w_key(key, part):
    return query_key_pair(key)[1].astype(jnp.bfloat16)


def levels(own_key, shape, shards, least, largest):
    def one(dim, blocks):
        draws = jax.random.uniform(jax.random.fold_in(jax.random.fold_in(own_key, 6), dim), (blocks,), jnp.float32, least / len(shards), largest / len(shards))
        return jnp.repeat(jnp.exp(draws), shape[dim] // blocks).reshape((-1,) + (1,) * (len(shape) - dim - 1))

    loudness = one(*shards[0])
    for cut in shards[1:]:
        loudness = loudness * one(*cut)
    return loudness


def normal_values(key, dims, scale, reach, cuts=(), held_as=jnp.bfloat16):
    values = jax.random.normal(key, dims, jnp.float32) * scale
    if len(cuts) > 0:
        values = levels(key, dims, cuts, -0.22, 0.18) * values
    return jnp.clip(values, min=-reach, max=reach).astype(held_as)


def setup_inputs(seed: int = 0, part: int = 0) -> dict:
    keys = jax.random.split(jax.random.key(seed), 13)
    own_keys = jax.random.split(jax.random.fold_in(keys[12], part), 13)
    features = normal_values(own_keys[0], (SNAPS, VERTS, D), 1.0, 6.0, ((0, 4), (1, 4)))
    adj_tiles = normal_values(own_keys[1], (SNAPS, BLOCKS, NBR_K, BLK, BLK), (NBR_K * BLK) ** -0.5, 0.25, ((0, 4), (1, 4)))
    neighbors = draw_neighbors(jax.random.fold_in(jax.random.fold_in(keys[12], part), 71), part)
    w_struct = normal_values(keys[3], (D, D), D ** -0.5, 0.375)
    pos_embed = normal_values(keys[4], (SNAPS, D), 0.5, 3.0)
    w_query = draw_w_query(jax.random.fold_in(keys[12], 71), part)
    w_key = draw_w_key(jax.random.fold_in(keys[12], 71), part)
    w_value = normal_values(keys[7], (D, D), D ** -0.5, 0.375)
    w_out = normal_values(keys[8], (D, D), D ** -0.5, 0.375)
    w_up = normal_values(keys[9], (D, FF), D ** -0.5, 0.375)
    up_bias = normal_values(keys[10], (FF,), 0.5, 3.0, (), jnp.float32)
    w_down = normal_values(keys[11], (FF, D), FF ** -0.5, 0.1875)
    return dict(features=features, adj_tiles=adj_tiles, neighbors=neighbors, w_struct=w_struct, pos_embed=pos_embed, w_query=w_query, w_key=w_key, w_value=w_value, w_out=w_out, w_up=w_up, up_bias=up_bias, w_down=w_down)


def structural(features, adj_tiles, neighbors, w_struct):

    def one_snapshot(packed):
        feat_now, tiles_now, nbr_now = packed
        projected = jnp.dot(feat_now, w_struct, preferred_element_type=jnp.float32).astype(jnp.bfloat16)
        projected = projected.reshape(BLOCKS, BLK, D)
        sources = projected[nbr_now]
        summed = jnp.einsum('bkij,bkjd->bid', tiles_now.astype(jnp.float32), sources.astype(jnp.float32))
        rows_in = feat_now.astype(jnp.float32).reshape(BLOCKS, BLK, D)
        return (rows_in + jax.nn.relu(summed)).astype(jnp.bfloat16).reshape(VERTS, D)
    return lax.map(one_snapshot, (features, adj_tiles, neighbors))

def temporal(zvals, w_query, w_key, w_value, w_out, w_up, up_bias, w_down):
    nsnap, nvert, width = zvals.shape
    queries = jnp.dot(zvals, w_query, preferred_element_type=jnp.float32).astype(jnp.bfloat16)
    keys_all = jnp.dot(zvals, w_key, preferred_element_type=jnp.float32).astype(jnp.bfloat16)
    values = jnp.dot(zvals, w_value, preferred_element_type=jnp.float32).astype(jnp.bfloat16)
    q_heads = queries.reshape(nsnap, nvert, HEADS, HEAD_DIM).astype(jnp.float32)
    k_heads = keys_all.reshape(nsnap, nvert, HEADS, HEAD_DIM).astype(jnp.float32)
    v_heads = values.reshape(nsnap, nvert, HEADS, HEAD_DIM).astype(jnp.float32)
    scores = jnp.einsum('tvhd,svhd->vhts', q_heads, k_heads) * (1.0 / math.sqrt(HEAD_DIM))
    causal = jnp.arange(nsnap)[:, None] >= jnp.arange(nsnap)[None, :]
    scores = jnp.where(causal, scores, -1e+30)
    peak = lax.optimization_barrier(jnp.max(scores, axis=-1, keepdims=True))
    expo = jnp.exp(scores - peak)
    probs = (expo / lax.optimization_barrier(jnp.sum(expo, axis=-1, keepdims=True))).astype(jnp.bfloat16)
    attended = jnp.einsum('vhts,svhd->tvhd', probs.astype(jnp.float32), v_heads)
    attended = attended.astype(jnp.bfloat16).reshape(nsnap, nvert, width)
    mixed = zvals.astype(jnp.float32) + jnp.dot(attended, w_out, preferred_element_type=jnp.float32)
    mixed_in = mixed.astype(jnp.bfloat16)
    hidden = jax.nn.relu(jnp.dot(mixed_in, w_up, preferred_element_type=jnp.float32) + up_bias).astype(jnp.bfloat16)
    return (mixed + jnp.dot(hidden, w_down, preferred_element_type=jnp.float32)).astype(jnp.bfloat16)

def reference(features, adj_tiles, neighbors, w_struct, pos_embed, w_query, w_key, w_value, w_out, w_up, up_bias, w_down):
    struct_out = structural(features, adj_tiles, neighbors, w_struct)
    zvals = (struct_out.astype(jnp.float32) + pos_embed.astype(jnp.float32)[:, None, :]).astype(jnp.bfloat16)
    nblocks = VERTS // BLK
    blocked = zvals.reshape(SNAPS, nblocks, BLK, D).transpose(1, 0, 2, 3)

    def one_block(zblock):
        return temporal(zblock, w_query, w_key, w_value, w_out, w_up, up_bias, w_down)
    result = lax.map(one_block, blocked)
    return result.transpose(1, 0, 2, 3).reshape(SNAPS, VERTS, D)
```

```python
import functools
import math

import jax
import jax.numpy as jnp
from jax import lax
from jax.experimental import pallas as pl
from jax.experimental.pallas import tpu as pltpu
from jax.sharding import PartitionSpec as P

HEADS = 8
LANES = 128
NEG = -1e30
F32 = jnp.float32
BF16 = jnp.bfloat16


def dot(a, b):
    return jnp.dot(a, b, preferred_element_type=F32)


def partner(me, d, n):
    return me ^ d if n & (n - 1) == 0 else (me + d) % n


def came_from(me, d, n):
    return me ^ d if n & (n - 1) == 0 else (me + n - d) % n


def named_mask(nbr_ref, t, first, cluster, blk_cl):
    last = nbr_ref.shape[1] - 1
    mask = jnp.int32(0)
    for i in range(blk_cl):
        g = nbr_ref[t, last, first + i] - cluster * blk_cl
        mask |= jnp.where((g >= 0) & (g < blk_cl), jnp.left_shift(1, g & 31), 0)
    return mask


def gather_kernel(most, n_clus, nbr_ref, feat_ref, *refs):
    snap_dev, blk_cl = feat_ref.shape[:2]
    outs, sems = refs[:-1], refs[-1]
    me = lax.axis_index("clus")
    copies = []
    for t in range(snap_dev):
        for d in range(1, n_clus):
            where_to = partner(me, d, n_clus)
            mask = named_mask(nbr_ref, t, where_to * blk_cl, me, blk_cl)
            picked = [jnp.int32(0)] * most
            count = jnp.int32(0)
            for b in range(blk_cl):
                bit = jnp.right_shift(mask, b) & 1
                for j in range(most):
                    picked[j] = jnp.where((bit == 1) & (count == j), b, picked[j])
                count += bit
            e = t * (n_clus - 1) + d - 1
            for j in range(most):
                copy = pltpu.make_async_copy(
                    feat_ref.at[t, picked[j]], outs[e].at[j], sems.at[e, j]
                )
                copy.start()
                copies.append(copy)
    for copy in copies:
        copy.wait()


def gather_blocks(nbr, feat, most, n_clus):
    snap_dev, _, block, width = feat.shape
    sets = snap_dev * (n_clus - 1)
    shape = (most, block, width)
    return pl.pallas_call(
        functools.partial(gather_kernel, most, n_clus),
        grid=(1,),
        out_shape=[pltpu.HBM(shape, BF16)] * sets,
        in_specs=[
            pl.BlockSpec(memory_space=pltpu.SMEM),
            pl.BlockSpec(memory_space=pl.ANY),
        ],
        out_specs=[pl.BlockSpec(shape, lambda g: (0, 0, 0))] * sets,
        scratch_shapes=[pltpu.SemaphoreType.DMA((sets, most))],
        cost_estimate=pl.CostEstimate(
            flops=0, bytes_accessed=2 * 2 * sets * most * block * width, transcendentals=0
        ),
        name="gather_blocks",
    )(nbr, feat)


def struct_kernel(dims, t, nbr_ref, feat_ref, *refs):
    n_clus, most, n_snap = dims
    remote = refs[: n_clus - 1]
    adj_ref, w_ref = refs[n_clus - 1 : n_clus + 1]
    outs = refs[n_clus + 1 : n_clus + 1 + n_snap]
    table, slots = refs[n_clus + 1 + n_snap :]
    g = pl.program_id(0)
    my_clus = lax.axis_index("clus")
    my_snap = lax.axis_index("snap") if n_snap > 1 else 0
    blk_cl, block, width = feat_ref.shape[1:]
    nbr_k = adj_ref.shape[2]
    first = my_clus * blk_cl

    @pl.when(g == 0)
    def _():
        for i in range(blk_cl):
            slots[i] = nbr_ref[t, nbr_k - 1, first + i] - first
        for d in range(1, n_clus):
            other = came_from(my_clus, d, n_clus)
            mask = named_mask(nbr_ref, t, first, other, blk_cl)
            for i in range(blk_cl):
                b = nbr_ref[t, nbr_k - 1, first + i] - other * blk_cl
                below = mask & (jnp.left_shift(1, b & 31) - 1)
                rank = jnp.int32(0)
                for _ in range(most):
                    rank += jnp.where(below != 0, 1, 0)
                    below &= below - 1
                slots[i] = jnp.where(
                    (b >= 0) & (b < blk_cl), blk_cl + (d - 1) * most + rank, slots[i]
                )
        w = w_ref[...]
        for b in range(blk_cl):
            table[b] = dot(feat_ref[0, b], w).astype(BF16)
        for d in range(n_clus - 1):
            for j in range(most):
                table[blk_cl + d * most + j] = dot(remote[d][j], w).astype(BF16)

    for d in range(n_snap):
        p = lax.rem(my_snap + d, n_snap) if n_snap > 1 else 0
        row = g * n_snap + p
        where = [nbr_ref[t, k, first + row] - first for k in range(nbr_k - 1)] + [slots[row]]
        tiles = jnp.concatenate([adj_ref[0, p, k] for k in range(nbr_k)], axis=1)
        total = dot(tiles, jnp.concatenate([table[slot] for slot in where], axis=0))
        outs[d][0] = (feat_ref[0, row].astype(F32) + jnp.maximum(total, 0.0)).astype(BF16)


def struct_phase(nbr, feat, remote, adj, w, t, n_snap):
    _, blk_cl, block, width = feat.shape
    nbr_k = adj.shape[2]
    n_clus = len(remote) + 1
    most = remote[0].shape[0] if remote else 0
    chunks = blk_cl // n_snap
    whole = lambda *shape: pl.BlockSpec(shape, lambda g: (0,) * len(shape))
    return pl.pallas_call(
        functools.partial(struct_kernel, (n_clus, most, n_snap), t),
        grid=(chunks,),
        out_shape=[pltpu.HBM((chunks, block, width), BF16)] * n_snap,
        in_specs=[
            pl.BlockSpec(memory_space=pltpu.SMEM),
            pl.BlockSpec((1, blk_cl, block, width), lambda g: (t, 0, 0, 0)),
        ]
        + [whole(most, block, width)] * (n_clus - 1)
        + [
            pl.BlockSpec((1, n_snap, nbr_k, block, block), lambda g: (t, g, 0, 0, 0)),
            whole(width, width),
        ],
        out_specs=[pl.BlockSpec((1, block, width), lambda g: (g, 0, 0))] * n_snap,
        scratch_shapes=[
            pltpu.VMEM((blk_cl + (n_clus - 1) * most, block, width), BF16),
            pltpu.SMEM((blk_cl,), jnp.int32),
        ],
        compiler_params=pltpu.CompilerParams(vmem_limit_bytes=24 << 20),
        cost_estimate=pl.CostEstimate(
            flops=2 * blk_cl * block * width * (2 * width + nbr_k * block),
            bytes_accessed=2 * blk_cl * block * (3 * width + nbr_k * block),
            transcendentals=0,
        ),
        name="struct_phase",
    )(nbr, feat, *remote, adj, w)


def temporal_kernel(n_snap, per, *refs):
    count = n_snap * per
    ins = refs[:count]
    pos_ref, wqkv_ref, wo_ref, wup_ref, bias_ref, wdown_ref = refs[count : count + 6]
    outs = refs[count + 6 : count + 6 + n_snap]
    zs, qkv, att, res = refs[count + 6 + n_snap :]
    me = lax.axis_index("snap")
    nsnap, nvert, width = zs.shape
    head_dim = width // HEADS
    for d in range(n_snap):
        src = lax.rem(me + n_snap - d, n_snap)
        for j in range(per):
            t = src * per + j
            zs[t] = (ins[d * per + j][0].astype(F32) + pos_ref[pl.ds(t, 1), :]).astype(BF16)

    for t in range(nsnap):
        qkv[t] = (
            lax.dot_general(
                wqkv_ref[...], zs[t], (((1,), (1,)), ((), ())), preferred_element_type=F32
            )
            .astype(BF16)
            .astype(F32)
        )

    def part(which, t):
        return qkv[t, which * width : (which + 1) * width, :].reshape(head_dim, HEADS, nvert)

    for t in range(nsnap):
        q = part(0, t)
        scores = [
            jnp.sum(q * part(1, s), axis=0) * (1.0 / math.sqrt(head_dim)) for s in range(t + 1)
        ]
        peak = functools.reduce(jnp.maximum, scores)
        expo = [jnp.exp(x - peak) for x in scores]
        total = functools.reduce(jnp.add, expo)
        acc = None
        for s in range(t + 1):
            prob = (expo[s] / total).astype(BF16).astype(F32)
            term = prob[None] * part(2, s)
            acc = term if acc is None else acc + term
        att[t] = acc.reshape(width, nvert).astype(BF16)

    group = max(1, 256 // nvert)
    for g in range(nsnap // group):
        some = slice(g * group, (g + 1) * group)
        z = zs[some].reshape(group * nvert, width)
        joined = jnp.concatenate([att[g * group + i] for i in range(group)], axis=1)
        mixed = z.astype(F32) + lax.dot_general(
            joined, wo_ref[...], (((0,), (0,)), ((), ())), preferred_element_type=F32
        )
        hidden = jnp.maximum(dot(mixed.astype(BF16), wup_ref[...]) + bias_ref[...], 0.0)
        out = mixed + dot(hidden.astype(BF16), wdown_ref[...])
        res[some] = out.astype(BF16).reshape(group, nvert, width)

    for d in range(n_snap):
        dst = lax.rem(me + d, n_snap)
        for j in range(per):
            outs[d][j] = res[dst * per + j]


def temporal_chunk(ins, chunk, weights, n_snap, per):
    pos, wqkv, wo, wup, bias, wdown = weights
    _, block, width = ins[0].shape
    nsnap = n_snap * per
    ff = wup.shape[1]
    whole = lambda x: pl.BlockSpec(x.shape, lambda g: (0,) * x.ndim)
    tokens = nsnap * block
    return pl.pallas_call(
        functools.partial(temporal_kernel, n_snap, per),
        grid=(1,),
        out_shape=[pltpu.HBM((per, block, width), BF16)] * n_snap,
        in_specs=[pl.BlockSpec((1, block, width), lambda g: (chunk, 0, 0))] * len(ins)
        + [whole(x) for x in weights],
        out_specs=[pl.BlockSpec((per, block, width), lambda g: (0, 0, 0))] * n_snap,
        scratch_shapes=[
            pltpu.VMEM((nsnap, block, width), BF16),
            pltpu.VMEM((nsnap, 3 * width, block), F32),
            pltpu.VMEM((nsnap, width, block), BF16),
            pltpu.VMEM((nsnap, block, width), BF16),
        ],
        compiler_params=pltpu.CompilerParams(vmem_limit_bytes=32 << 20),
        cost_estimate=pl.CostEstimate(
            flops=2 * tokens * width * (4 * width + 2 * ff),
            bytes_accessed=4 * tokens * width + 2 * width * (4 * width + 2 * ff),
            transcendentals=tokens * HEADS * nsnap,
        ),
        name="temporal_chunk",
    )(*ins, *weights)


def head_minor(w):
    width = w.shape[0]
    return w.T.reshape(HEADS, width // HEADS, width).transpose(1, 0, 2).reshape(width, width)


def shift(x, d, n):
    return lax.ppermute(x, "snap", [(i, (i + d) % n) for i in range(n)])


def temporal_fast(sent, weights, n_snap):
    per = len(sent)
    chunks, block, width = sent[0][0].shape
    got = [
        [sent[t][d] if d == 0 else shift(sent[t][d], d, n_snap) for d in range(n_snap)]
        for t in range(per)
    ]
    out = jnp.zeros((per, chunks * n_snap * block, width), BF16)
    me = lax.axis_index("snap")
    for c in range(chunks):
        ins = [got[j][d] for d in range(n_snap) for j in range(per)]
        res = temporal_chunk(ins, c, weights, n_snap, per)
        for d in range(n_snap):
            back = res[d] if d == 0 else shift(res[d], d, n_snap)
            src = (me + n_snap - d) % n_snap
            out = lax.dynamic_update_slice_in_dim(out, back, (c * n_snap + src) * block, 1)
    return out


def temporal_plain(zvals, w_query, w_key, w_value, w_out, w_up, up_bias, w_down):
    nsnap, nvert, width = zvals.shape
    head_dim = width // HEADS
    heads = (nsnap, nvert, HEADS, head_dim)
    q_heads = dot(zvals, w_query).astype(BF16).reshape(heads)
    k_heads = dot(zvals, w_key).astype(BF16).reshape(heads)
    v_heads = dot(zvals, w_value).astype(BF16).reshape(heads)
    scores = jnp.einsum("tvhd,svhd->vhts", q_heads, k_heads, preferred_element_type=F32)
    scores = scores * (1.0 / math.sqrt(head_dim))
    causal = jnp.arange(nsnap)[:, None] >= jnp.arange(nsnap)[None, :]
    scores = jnp.where(causal, scores, NEG)
    peak = jnp.max(scores, axis=-1, keepdims=True)
    expo = jnp.exp(scores - peak)
    probs = (expo / jnp.sum(expo, axis=-1, keepdims=True)).astype(BF16)
    attended = jnp.einsum("vhts,svhd->tvhd", probs, v_heads, preferred_element_type=F32)
    attended = attended.astype(BF16).reshape(nsnap, nvert, width)
    mixed = zvals.astype(F32) + dot(attended, w_out)
    hidden = jax.nn.relu(dot(mixed.astype(BF16), w_up) + up_bias).astype(BF16)
    return (mixed + dot(hidden, w_down)).astype(BF16)


def on_device(
    features,
    adj_tiles,
    neighbors,
    w_struct,
    pos_embed,
    w_query,
    w_key,
    w_value,
    w_out,
    w_up,
    up_bias,
    w_down,
):
    snap_dev, vert_cl, width = features.shape
    blk_cl, nbr_k, block = adj_tiles.shape[1:4]
    n_clus, n_snap = lax.axis_size("clus"), lax.axis_size("snap")
    most = 4
    nbr = neighbors.transpose(0, 2, 1)
    feat = features.reshape(snap_dev, blk_cl, block, width)
    sets = gather_blocks(nbr, feat, most, n_clus)
    remote = []
    for t in range(snap_dev):
        remote.append(
            [
                lax.ppermute(
                    sets[t * (n_clus - 1) + d - 1],
                    "clus",
                    [(i, partner(i, d, n_clus)) for i in range(n_clus)],
                )
                for d in range(1, n_clus)
            ]
        )
    fast = snap_dev * n_snap <= 8 and blk_cl % n_snap == 0 and block % LANES == 0
    groups = n_snap if fast else 1
    sent = [
        struct_phase(nbr, feat, remote[t], adj_tiles, w_struct, t, groups)
        for t in range(snap_dev)
    ]
    if fast:
        weights = (
            pos_embed.astype(F32),
            jnp.concatenate([head_minor(w_query), head_minor(w_key), head_minor(w_value)], 0),
            w_out.reshape(HEADS, width // HEADS, width)
            .transpose(1, 0, 2)
            .reshape(width, width),
            w_up,
            up_bias.reshape(1, -1),
            w_down,
        )
        return temporal_fast(sent, weights, n_snap)
    vert_dev = vert_cl // n_snap
    struct_out = jnp.stack([s[0].reshape(n_snap, vert_dev, width) for s in sent])
    inputs = lax.all_to_all(struct_out, "snap", split_axis=1, concat_axis=0, tiled=True)[:, 0]
    zvals = (inputs.astype(F32) + pos_embed.astype(F32)[:, None, :]).astype(BF16)
    result = temporal_plain(zvals, w_query, w_key, w_value, w_out, w_up, up_bias, w_down)
    returned = lax.all_to_all(
        result[:, None], "snap", split_axis=0, concat_axis=1, tiled=True
    )
    return returned.reshape(snap_dev, vert_cl, width)


def solution(mesh):
    placed = (
        P(("grp", "snap"), "clus", None),
        P(("grp", "snap"), "clus", None, None, None),
        P(("grp", "snap"), None, None),
        P(),
        P(),
        P(),
        P(),
        P(),
        P(),
        P(),
        P(),
        P(),
    )
    return jax.shard_map(
        on_device,
        mesh=mesh,
        in_specs=placed,
        out_specs=P(("grp", "snap"), "clus", None),
        check_vma=False,
    )
```

```python
import functools
import math

import jax
import jax.numpy as jnp
from jax import lax
from jax.experimental import pallas as pl
from jax.experimental.pallas import tpu as pltpu
from jax.sharding import PartitionSpec as P

HEADS = 8
LANES = 128
ALONE, ROOM = 60, (57, 46)
GATHER_US, GATE_US, NEAR_US, FAR_US, TEMPORAL_US, PLACE_US = 3, 0.5, 3, 2, 3, 1
NEG = -1e30
F32 = jnp.float32
BF16 = jnp.bfloat16


def cost(us):
    return pl.CostEstimate(flops=0, bytes_accessed=int(us * 3.0e4), transcendentals=0)


def dot(a, b):
    return jnp.dot(a, b, preferred_element_type=F32)


def partner(me, d, n):
    return me ^ d if n & (n - 1) == 0 else (me + d) % n


def came_from(me, d, n):
    return me ^ d if n & (n - 1) == 0 else (me + n - d) % n


def named_mask(nbr_ref, t, first, cluster, blk_cl):
    last = nbr_ref.shape[1] - 1
    mask = jnp.int32(0)
    for i in range(blk_cl):
        g = nbr_ref[t, last, first + i] - cluster * blk_cl
        mask |= jnp.where((g >= 0) & (g < blk_cl), jnp.left_shift(1, g & 31), 0)
    return mask


def gather_kernel(t, most, n_clus, after_ref, nbr_ref, feat_ref, *refs):
    blk_cl = feat_ref.shape[1]
    outs, done_ref, sems = refs[:-2], refs[-2], refs[-1]
    done_ref[0] = jnp.int32(0)
    me = lax.axis_index("clus")
    copies = []
    for d in range(1, n_clus):
        mask = named_mask(nbr_ref, t, partner(me, d, n_clus) * blk_cl, me, blk_cl)
        picked = [jnp.int32(0)] * most
        count = jnp.int32(0)
        for b in range(blk_cl):
            bit = jnp.right_shift(mask, b) & 1
            for j in range(most):
                picked[j] = jnp.where((bit == 1) & (count == j), b, picked[j])
            count += bit
        for j in range(most):
            copy = pltpu.make_async_copy(
                feat_ref.at[t, picked[j]], outs[d - 1].at[j], sems.at[d - 1, j]
            )
            copy.start()
            copies.append(copy)
    for copy in copies:
        copy.wait()


def gather_blocks(after, nbr, feat, t, most, n_clus):
    _, _, block, width = feat.shape
    shape = (most, block, width)
    *out, done = pl.pallas_call(
        functools.partial(gather_kernel, t, most, n_clus),
        grid=(1,),
        out_shape=[pltpu.HBM(shape, BF16)] * (n_clus - 1)
        + [jax.ShapeDtypeStruct((1,), jnp.int32)],
        in_specs=[
            pl.BlockSpec(memory_space=pltpu.SMEM),
            pl.BlockSpec(memory_space=pltpu.SMEM),
            pl.BlockSpec(memory_space=pltpu.HBM),
        ],
        out_specs=[pl.BlockSpec(shape, lambda g: (0, 0, 0))] * (n_clus - 1)
        + [pl.BlockSpec(memory_space=pltpu.SMEM)],
        scratch_shapes=[pltpu.SemaphoreType.DMA((n_clus - 1, most))],
        compiler_params=pltpu.CompilerParams(vmem_limit_bytes=ALONE << 20),
        cost_estimate=cost(GATHER_US),
        name="gather_blocks",
    )(after, nbr, feat)
    return out, done


def gate_kernel(*refs):
    pass


def gate(after, xs):
    hbm = pl.BlockSpec(memory_space=pltpu.HBM)
    return pl.pallas_call(
        gate_kernel,
        out_shape=[pltpu.HBM(x.shape, x.dtype) for x in xs],
        in_specs=[pl.BlockSpec(memory_space=pl.ANY)] * len(after) + [hbm] * len(xs),
        out_specs=[hbm] * len(xs),
        input_output_aliases={i + len(after): i for i in range(len(xs))},
        compiler_params=pltpu.CompilerParams(vmem_limit_bytes=1 << 20),
        cost_estimate=cost(GATE_US),
        name="gate",
    )(*after, *xs)


def near_kernel(
    t, n_clus, most, after_ref, nbr_ref, feat_ref, adj_ref, w_ref, acc_ref, own, tiles, slots, table, sems
):
    my_clus = lax.axis_index("clus")
    blk_cl, block, width = own.shape
    nbr_k = tiles.shape[1]
    pieces = sems.shape[1]
    rows = blk_cl // pieces
    first = my_clus * blk_cl
    copies = []
    for source, target in ((feat_ref, own), (adj_ref, tiles)):
        for i in range(pieces):
            some = pl.ds(i * rows, rows)
            copies.append(
                pltpu.make_async_copy(
                    source.at[t, some], target.at[some], sems.at[len(copies) // pieces, i]
                )
            )
            copies[-1].start()
    for i in range(blk_cl):
        slots[i] = (n_clus - 1) * most
    for d in range(1, n_clus):
        other = came_from(my_clus, d, n_clus)
        mask = named_mask(nbr_ref, t, first, other, blk_cl)
        for i in range(blk_cl):
            b = nbr_ref[t, nbr_k - 1, first + i] - other * blk_cl
            below = mask & (jnp.left_shift(1, b & 31) - 1)
            rank = jnp.int32(0)
            for _ in range(most):
                rank += jnp.where(below != 0, 1, 0)
                below &= below - 1
            slots[i] = jnp.where((b >= 0) & (b < blk_cl), (d - 1) * most + rank, slots[i])
    w = w_ref[...]
    for i in range(pieces):
        copies[i].wait()
        some = own[i * rows : (i + 1) * rows].reshape(rows * block, width)
        table[i * rows : (i + 1) * rows] = dot(some, w).astype(BF16).reshape(rows, block, width)
    table[blk_cl] = jnp.zeros((block, width), BF16)
    for row in range(blk_cl):
        if row % rows == 0:
            copies[pieces + row // rows].wait()
        where = [nbr_ref[t, k, first + row] - first for k in range(nbr_k)]
        where[-1] = jnp.where((where[-1] >= 0) & (where[-1] < blk_cl), where[-1], blk_cl)
        wide = jnp.concatenate([tiles[row, k] for k in range(nbr_k)], axis=1)
        acc_ref[row] = dot(wide, jnp.concatenate([table[slot] for slot in where], axis=0))


def near_sum(after, nbr, feat, adj, w, t, n_clus, most, room):
    _, blk_cl, block, width = feat.shape
    nbr_k = adj.shape[2]
    pieces = 4 if blk_cl % 4 == 0 else 1
    vmem = pl.BlockSpec(memory_space=pltpu.VMEM)
    smem = pl.BlockSpec(memory_space=pltpu.SMEM)
    hbm = pl.BlockSpec(memory_space=pltpu.HBM)
    return pl.pallas_call(
        functools.partial(near_kernel, t, n_clus, most),
        out_shape=[
            pltpu.VMEM((blk_cl, block, width), F32),
            pltpu.VMEM((blk_cl, block, width), BF16),
            pltpu.VMEM((blk_cl, nbr_k, block, block), BF16),
            jax.ShapeDtypeStruct((blk_cl,), jnp.int32),
        ],
        in_specs=[smem, smem, hbm, hbm, vmem],
        out_specs=[vmem, vmem, vmem, smem],
        scratch_shapes=[
            pltpu.VMEM((blk_cl + 1, block, width), BF16),
            pltpu.SemaphoreType.DMA((2, pieces)),
        ],
        compiler_params=pltpu.CompilerParams(vmem_limit_bytes=room << 20),
        cost_estimate=cost(NEAR_US),
        name="near_sum",
    )(after, nbr, feat, adj, w)


def far_kernel(n_snap, parts, slots, acc_ref, own, tiles, w_ref, *refs):
    n_out = n_snap * len(parts)
    remote, outs = refs[: -n_out - 4], refs[-n_out - 4 : -4]
    done_ref, table, held, sems = refs[-4:]
    done_ref[0] = jnp.int32(0)
    my_snap = lax.axis_index("snap") if n_snap > 1 else jnp.int32(0)
    most, block, width = remote[0].shape
    w = w_ref[...]
    for d, ref in enumerate(remote):
        some = dot(ref[...].reshape(most * block, width), w).astype(BF16)
        table[d * most : (d + 1) * most] = some.reshape(most, block, width)
    table[len(remote) * most] = jnp.zeros((block, width), BF16)
    copies = []
    for e, (lo, hi) in enumerate(parts):
        for d in list(range(1, n_snap)) + [0]:
            p = partner(my_snap, d, n_snap)
            for g in range(lo, hi):
                row = g * n_snap + p
                total = acc_ref[row] + dot(tiles[row, tiles.shape[1] - 1], table[slots[row]])
                total = (own[row].astype(F32) + jnp.maximum(total, 0.0)).astype(BF16)
                if d == 0:
                    outs[e * n_snap][g - lo] = total
                else:
                    held[d - 1, g] = total
            if d > 0:
                copies.append(
                    pltpu.make_async_copy(
                        held.at[d - 1, lo:hi], outs[e * n_snap + d], sems.at[e, d - 1]
                    )
                )
                copies[-1].start()
    for copy in copies:
        copy.wait()


def far_sum(near, remote, w, n_snap, parts):
    acc, own, tiles, slots = near
    most, block, width = remote[0].shape
    vmem = pl.BlockSpec(memory_space=pltpu.VMEM)
    hbm = pl.BlockSpec(memory_space=pltpu.HBM)
    shapes = [(hi - lo, block, width) for lo, hi in parts]
    *out, done = pl.pallas_call(
        functools.partial(far_kernel, n_snap, parts),
        out_shape=[
            (pltpu.HBM if d else pltpu.VMEM)(shape, BF16) for shape in shapes for d in range(n_snap)
        ]
        + [jax.ShapeDtypeStruct((1,), jnp.int32)],
        in_specs=[pl.BlockSpec(memory_space=pltpu.SMEM)] + [vmem] * (4 + len(remote)),
        out_specs=[hbm if d else vmem for _ in shapes for d in range(n_snap)]
        + [pl.BlockSpec(memory_space=pltpu.SMEM)],
        scratch_shapes=[
            pltpu.VMEM((len(remote) * most + 1, block, width), BF16),
            pltpu.VMEM((max(n_snap - 1, 1), parts[-1][1], block, width), BF16),
            pltpu.SemaphoreType.DMA((len(parts), max(n_snap - 1, 1))),
        ],
        compiler_params=pltpu.CompilerParams(vmem_limit_bytes=8 << 20),
        cost_estimate=cost(FAR_US),
        name="far_sum",
    )(slots, acc, own, tiles, w, *remote)
    return [out[e * n_snap : (e + 1) * n_snap] for e in range(len(parts))], done


def prepare_kernel(after_ref, pos_ref, wq_ref, wk_ref, wv_ref, wo_ref, pos, wqkv, wo):
    width = wo.shape[0]
    head_dim = width // HEADS
    to = lax.broadcasted_iota(jnp.int32, (width, width), 0)
    source = lax.broadcasted_iota(jnp.int32, (width, width), 1)
    named = (to & (HEADS - 1)) * head_dim + jnp.right_shift(to, HEADS.bit_length() - 1)
    order = jnp.where(source == named, 1.0, 0.0).astype(BF16)
    for i, ref in enumerate((wq_ref, wk_ref, wv_ref)):
        turned = lax.dot_general(
            order, ref[...], (((1,), (1,)), ((), ())), preferred_element_type=F32
        )
        wqkv[i * width : (i + 1) * width] = turned.astype(BF16)
    wo[...] = dot(order, wo_ref[...]).astype(BF16)
    pos[...] = pos_ref[...].astype(F32)


def prepare(after, pos, wq, wk, wv, wo):
    width = wo.shape[0]
    vmem = pl.BlockSpec(memory_space=pltpu.VMEM)
    return pl.pallas_call(
        prepare_kernel,
        out_shape=[
            pltpu.VMEM(pos.shape, F32),
            pltpu.VMEM((3 * width, width), BF16),
            pltpu.VMEM((width, width), BF16),
        ],
        in_specs=[pl.BlockSpec(memory_space=pltpu.SMEM)] + [vmem] * 5,
        out_specs=[vmem] * 3,
        compiler_params=pltpu.CompilerParams(vmem_limit_bytes=4 << 20),
        cost_estimate=cost(1),
        name="prepare",
    )(after, pos, wq, wk, wv, wo)


def temporal_kernel(n_snap, per, blocks, chunk, *refs):
    count = n_snap * per
    ins = refs[:count]
    pos_ref, wqkv_ref, wo_ref, wup_ref, bias_ref, wdown_ref = refs[count : count + 6]
    outs = refs[-5 - n_snap : -5]
    raw, zs, qkv, att, out_sems = refs[-5:]
    me = lax.axis_index("snap")
    nsnap, nvert, width = zs.shape
    head_dim = width // HEADS
    for d in range(n_snap):
        for j in range(per):
            i = d * per + j
            raw[came_from(me, d, n_snap) * per + j] = ins[i][blocks[i]]

    for t in range(nsnap):
        zs[t] = (raw[t].astype(F32) + pos_ref[t : t + 1, :]).astype(BF16)
        qkv[t] = (
            lax.dot_general(
                wqkv_ref[...], zs[t], (((1,), (1,)), ((), ())), preferred_element_type=F32
            )
            .astype(BF16)
            .astype(F32)
        )

    def part(which, t):
        return qkv[t, which * width : (which + 1) * width, :].reshape(head_dim, HEADS, nvert)

    for t in range(nsnap):
        q = part(0, t)
        scores = [
            jnp.sum(q * part(1, s), axis=0) * (1.0 / math.sqrt(head_dim)) for s in range(t + 1)
        ]
        peak = functools.reduce(jnp.maximum, scores)
        expo = [jnp.exp(x - peak) for x in scores]
        total = functools.reduce(jnp.add, expo)
        acc = None
        for s in range(t + 1):
            prob = (expo[s] / total).astype(BF16).astype(F32)
            term = prob[None] * part(2, s)
            acc = term if acc is None else acc + term
        att[t] = acc.reshape(width, nvert).astype(BF16)

    def send(d, first):
        target = outs[d]
        if d == 0:
            target = target.at[:, pl.ds((chunk * n_snap + me) * nvert, nvert)]
        return pltpu.make_async_copy(raw.at[pl.ds(first, per)], target, out_sems.at[d])

    for g in range(n_snap):
        some = slice(g * per, (g + 1) * per)
        z = zs[some].reshape(per * nvert, width)
        joined = jnp.concatenate([att[g * per + j] for j in range(per)], axis=1)
        mixed = z.astype(F32) + lax.dot_general(
            joined, wo_ref[...], (((0,), (0,)), ((), ())), preferred_element_type=F32
        )
        hidden = jnp.maximum(dot(mixed.astype(BF16), wup_ref[...]) + bias_ref[...], 0.0)
        out = mixed + dot(hidden.astype(BF16), wdown_ref[...])
        raw[some] = out.astype(BF16).reshape(per, nvert, width)
        for d in range(n_snap):

            @pl.when(partner(me, d, n_snap) == g)
            def _():
                send(d, g * per).start()

    for d in range(n_snap):
        send(d, partner(me, d, n_snap) * per).wait()


def temporal_chunk(ins, blocks, weights, n_snap, per, chunk, chunks, result, waits):
    _, block, width = ins[0].shape
    nsnap = n_snap * per
    vmem = pl.BlockSpec(memory_space=pltpu.VMEM)
    hbm = pl.BlockSpec(memory_space=pltpu.HBM)
    before = [] if result is None else [result]
    n_in = len(ins) + len(weights)
    return pl.pallas_call(
        functools.partial(temporal_kernel, n_snap, per, blocks, chunk),
        out_shape=[pltpu.HBM((per, chunks * n_snap * block, width), BF16)]
        + [pltpu.HBM((per, block, width), BF16)] * (n_snap - 1),
        in_specs=[vmem] * (len(ins) + len(weights)) + [hbm] * len(before + waits),
        out_specs=[hbm] * n_snap,
        input_output_aliases={n_in: 0} if before else {},
        scratch_shapes=[
            pltpu.VMEM((nsnap, block, width), BF16),
            pltpu.VMEM((nsnap, block, width), BF16),
            pltpu.VMEM((nsnap, 3 * width, block), F32),
            pltpu.VMEM((nsnap, width, block), BF16),
            pltpu.SemaphoreType.DMA((n_snap,)),
        ],
        compiler_params=pltpu.CompilerParams(vmem_limit_bytes=14 << 20),
        cost_estimate=cost(TEMPORAL_US),
        name="temporal_chunk",
    )(*ins, *weights, *before, *waits)


def place_kernel(n_snap, chunk, *refs):
    blocks, (_, out_ref, sems) = refs[: n_snap - 1], refs[n_snap - 1 :]
    block = blocks[0].shape[1]
    me = lax.axis_index("snap")
    copies = []
    for d in range(1, n_snap):
        row = (chunk * n_snap + came_from(me, d, n_snap)) * block
        copies.append(
            pltpu.make_async_copy(blocks[d - 1], out_ref.at[:, pl.ds(row, block)], sems.at[d - 1])
        )
        copies[-1].start()
    for copy in copies:
        copy.wait()


def place(result, blocks, n_snap, chunk):
    hbm = pl.BlockSpec(memory_space=pltpu.HBM)
    return pl.pallas_call(
        functools.partial(place_kernel, n_snap, chunk),
        out_shape=pltpu.HBM(result.shape, result.dtype),
        in_specs=[pl.BlockSpec(memory_space=pltpu.VMEM)] * len(blocks) + [hbm],
        out_specs=hbm,
        input_output_aliases={len(blocks): 0},
        scratch_shapes=[pltpu.SemaphoreType.DMA((n_snap - 1,))],
        compiler_params=pltpu.CompilerParams(vmem_limit_bytes=1 << 20),
        cost_estimate=cost(PLACE_US),
        name="place",
    )(*blocks, result)


def shift(x, d, n):
    return lax.ppermute(x, "snap", [(i, partner(i, d, n)) for i in range(n)])


def temporal_fast(got, parts, weights, n_snap, first):
    per = len(got)
    chunks = parts[0][-1][1]
    result, backs = None, []
    for c in range(chunks):
        ins, blocks = [], []
        for d in range(n_snap):
            for j in range(per):
                e = [lo <= c < hi for lo, hi in parts[j]].index(True)
                ins.append(got[j][e][d])
                blocks.append(c - parts[j][e][0])
        result, *sent = temporal_chunk(
            ins, blocks, weights, n_snap, per, c, chunks, result, first if c == 0 else []
        )
        backs.append([shift(x, d + 1, n_snap) for d, x in enumerate(sent)])
        if c > 0:
            result = place(result, backs[c - 1], n_snap, c - 1)
    return place(result, backs[-1], n_snap, chunks - 1)


def temporal_plain(zvals, w_query, w_key, w_value, w_out, w_up, up_bias, w_down):
    nsnap, nvert, width = zvals.shape
    head_dim = width // HEADS
    heads = (nsnap, nvert, HEADS, head_dim)
    q_heads = dot(zvals, w_query).astype(BF16).reshape(heads)
    k_heads = dot(zvals, w_key).astype(BF16).reshape(heads)
    v_heads = dot(zvals, w_value).astype(BF16).reshape(heads)
    scores = jnp.einsum("tvhd,svhd->vhts", q_heads, k_heads, preferred_element_type=F32)
    scores = scores * (1.0 / math.sqrt(head_dim))
    causal = jnp.arange(nsnap)[:, None] >= jnp.arange(nsnap)[None, :]
    scores = jnp.where(causal, scores, NEG)
    peak = jnp.max(scores, axis=-1, keepdims=True)
    expo = jnp.exp(scores - peak)
    probs = (expo / jnp.sum(expo, axis=-1, keepdims=True)).astype(BF16)
    attended = jnp.einsum("vhts,svhd->tvhd", probs, v_heads, preferred_element_type=F32)
    attended = attended.astype(BF16).reshape(nsnap, nvert, width)
    mixed = zvals.astype(F32) + dot(attended, w_out)
    hidden = jax.nn.relu(dot(mixed.astype(BF16), w_up) + up_bias).astype(BF16)
    return (mixed + dot(hidden, w_down)).astype(BF16)


def on_device(
    features,
    adj_tiles,
    neighbors,
    w_struct,
    pos_embed,
    w_query,
    w_key,
    w_value,
    w_out,
    w_up,
    up_bias,
    w_down,
):
    snap_dev, vert_cl, width = features.shape
    blk_cl, nbr_k, block = adj_tiles.shape[1:4]
    n_clus, n_snap = lax.axis_size("clus"), lax.axis_size("snap")
    most = 4
    nbr = neighbors.transpose(0, 2, 1)
    feat = features.reshape(snap_dev, blk_cl, block, width)
    fast = snap_dev * n_snap <= 8 and blk_cl % n_snap == 0 and block % LANES == 0
    groups = n_snap if fast else 1
    chunks = blk_cl // groups
    done = jnp.zeros((1,), jnp.int32)
    sets = []
    for t in range(snap_dev):
        some, done = gather_blocks(done, nbr, feat, t, most, n_clus)
        sets.append(some)
    got, parts, prepared = [], [], None
    for t in range(snap_dev):
        near = near_sum(done, nbr, feat, adj_tiles, w_struct, t, n_clus, most, ROOM[min(t, 1)])
        if t == 0:
            for later in range(1, snap_dev):
                sets[later] = gate(near[-1:], sets[later])
        remote = [
            lax.ppermute(x, "clus", [(i, partner(i, d + 1, n_clus)) for i in range(n_clus)])
            for d, x in enumerate(sets[t])
        ]
        last = t == snap_dev - 1 and fast and chunks > 1
        parts.append([(0, 1), (1, chunks)] if last else [(0, chunks)])
        sent, done = far_sum(near, remote, w_struct, groups, parts[-1])
        got.append([])
        for e, part in enumerate(sent):
            if t > 0 and n_snap > 2:
                waits = got[-2][-1][1:3] if e == 0 else got[-2][-1][3:] + got[-1][-1][1:2]
                part[1:] = gate(waits, part[1:])
            got[-1].append([x if d == 0 else shift(x, d, n_snap) for d, x in enumerate(part)])
        if t == 0 and fast:
            prepared = prepare(done, pos_embed, w_query, w_key, w_value, w_out)
    if fast:
        weights = (*prepared, w_up, up_bias.reshape(1, -1), w_down)
        return temporal_fast(got, parts, weights, n_snap, sent[-1][1:2])
    vert_dev = vert_cl // n_snap
    struct_out = jnp.stack([g[0][0].reshape(n_snap, vert_dev, width) for g in got])
    inputs = lax.all_to_all(struct_out, "snap", split_axis=1, concat_axis=0, tiled=True)[:, 0]
    zvals = (inputs.astype(F32) + pos_embed.astype(F32)[:, None, :]).astype(BF16)
    result = temporal_plain(zvals, w_query, w_key, w_value, w_out, w_up, up_bias, w_down)
    returned = lax.all_to_all(
        result[:, None], "snap", split_axis=0, concat_axis=1, tiled=True
    )
    return returned.reshape(snap_dev, vert_cl, width)


def solution(mesh):
    placed = (
        P(("grp", "snap"), "clus", None),
        P(("grp", "snap"), "clus", None, None, None),
        P(("grp", "snap"), None, None),
        P(),
        P(),
        P(),
        P(),
        P(),
        P(),
        P(),
        P(),
        P(),
    )
    return jax.shard_map(
        on_device,
        mesh=mesh,
        in_specs=placed,
        out_specs=P(("grp", "snap"), "clus", None),
        check_vma=False,
    )
```

```python
import functools
import math

import jax
import jax.numpy as jnp
from jax import lax
from jax.experimental import pallas as pl
from jax.experimental.pallas import tpu as pltpu
from jax.sharding import PartitionSpec as P

HEADS = 8
LANES = 128
LAG = 2
ALONE, ROOM = 60, (57, 46)
GATHER_US, GATE_US, NEAR_US, FAR_US, TEMPORAL_US, PLACE_US = 3, 0.5, 3, 2, 3, 1
NEG = -1e30
F32 = jnp.float32
BF16 = jnp.bfloat16


def cost(us):
    return pl.CostEstimate(flops=0, bytes_accessed=int(us * 3.0e4), transcendentals=0)


def dot(a, b):
    return jnp.dot(a, b, preferred_element_type=F32)


def partner(me, d, n):
    return me ^ d if n & (n - 1) == 0 else (me + d) % n


def came_from(me, d, n):
    return me ^ d if n & (n - 1) == 0 else (me + n - d) % n


def named_mask(nbr_ref, t, first, cluster, blk_cl):
    last = nbr_ref.shape[1] - 1
    mask = jnp.int32(0)
    for i in range(blk_cl):
        g = nbr_ref[t, last, first + i] - cluster * blk_cl
        mask |= jnp.where((g >= 0) & (g < blk_cl), jnp.left_shift(1, g & 31), 0)
    return mask


def gather_kernel(t, most, n_clus, after_ref, nbr_ref, feat_ref, *refs):
    blk_cl = feat_ref.shape[1]
    outs, done_ref, sems = refs[:-2], refs[-2], refs[-1]
    done_ref[0] = jnp.int32(0)
    me = lax.axis_index("clus")
    copies = []
    for d in range(1, n_clus):
        mask = named_mask(nbr_ref, t, partner(me, d, n_clus) * blk_cl, me, blk_cl)
        picked = [jnp.int32(0)] * most
        count = jnp.int32(0)
        for b in range(blk_cl):
            bit = jnp.right_shift(mask, b) & 1
            for j in range(most):
                picked[j] = jnp.where((bit == 1) & (count == j), b, picked[j])
            count += bit
        for j in range(most):
            copy = pltpu.make_async_copy(
                feat_ref.at[t, picked[j]], outs[d - 1].at[j], sems.at[d - 1, j]
            )
            copy.start()
            copies.append(copy)
    for copy in copies:
        copy.wait()


def gather_blocks(after, nbr, feat, t, most, n_clus):
    _, _, block, width = feat.shape
    shape = (most, block, width)
    *out, done = pl.pallas_call(
        functools.partial(gather_kernel, t, most, n_clus),
        grid=(1,),
        out_shape=[pltpu.HBM(shape, BF16)] * (n_clus - 1)
        + [jax.ShapeDtypeStruct((1,), jnp.int32)],
        in_specs=[
            pl.BlockSpec(memory_space=pltpu.SMEM),
            pl.BlockSpec(memory_space=pltpu.SMEM),
            pl.BlockSpec(memory_space=pltpu.HBM),
        ],
        out_specs=[pl.BlockSpec(shape, lambda g: (0, 0, 0))] * (n_clus - 1)
        + [pl.BlockSpec(memory_space=pltpu.SMEM)],
        scratch_shapes=[pltpu.SemaphoreType.DMA((n_clus - 1, most))],
        compiler_params=pltpu.CompilerParams(vmem_limit_bytes=ALONE << 20),
        cost_estimate=cost(GATHER_US),
        name="gather_blocks",
    )(after, nbr, feat)
    return out, done


def gate_kernel(*refs):
    refs[-1][0] = jnp.int32(0)


def gate(after, xs):
    hbm = pl.BlockSpec(memory_space=pltpu.HBM)
    *out, done = pl.pallas_call(
        gate_kernel,
        out_shape=[pltpu.HBM(x.shape, x.dtype) for x in xs]
        + [jax.ShapeDtypeStruct((1,), jnp.int32)],
        in_specs=[pl.BlockSpec(memory_space=pl.ANY)] * len(after) + [hbm] * len(xs),
        out_specs=[hbm] * len(xs) + [pl.BlockSpec(memory_space=pltpu.SMEM)],
        input_output_aliases={i + len(after): i for i in range(len(xs))},
        compiler_params=pltpu.CompilerParams(vmem_limit_bytes=1 << 20),
        cost_estimate=cost(GATE_US),
        name="gate",
    )(*after, *xs)
    return out, done


def near_kernel(
    t, n_clus, most, after_ref, nbr_ref, feat_ref, adj_ref, w_ref, acc_ref, own, tiles, slots, table, sems
):
    my_clus = lax.axis_index("clus")
    blk_cl, block, width = own.shape
    nbr_k = tiles.shape[1]
    pieces = sems.shape[1]
    rows = blk_cl // pieces
    first = my_clus * blk_cl
    copies = []
    for source, target in ((feat_ref, own), (adj_ref, tiles)):
        for i in range(pieces):
            some = pl.ds(i * rows, rows)
            copies.append(
                pltpu.make_async_copy(
                    source.at[t, some], target.at[some], sems.at[len(copies) // pieces, i]
                )
            )
            copies[-1].start()
    for i in range(blk_cl):
        slots[i] = (n_clus - 1) * most
    for d in range(1, n_clus):
        other = came_from(my_clus, d, n_clus)
        mask = named_mask(nbr_ref, t, first, other, blk_cl)
        for i in range(blk_cl):
            b = nbr_ref[t, nbr_k - 1, first + i] - other * blk_cl
            below = mask & (jnp.left_shift(1, b & 31) - 1)
            rank = jnp.int32(0)
            for _ in range(most):
                rank += jnp.where(below != 0, 1, 0)
                below &= below - 1
            slots[i] = jnp.where((b >= 0) & (b < blk_cl), (d - 1) * most + rank, slots[i])
    w = w_ref[...]
    for i in range(pieces):
        copies[i].wait()
        some = own[i * rows : (i + 1) * rows].reshape(rows * block, width)
        table[i * rows : (i + 1) * rows] = dot(some, w).astype(BF16).reshape(rows, block, width)
    table[blk_cl] = jnp.zeros((block, width), BF16)
    for row in range(blk_cl):
        if row % rows == 0:
            copies[pieces + row // rows].wait()
        where = [nbr_ref[t, k, first + row] - first for k in range(nbr_k)]
        where[-1] = jnp.where((where[-1] >= 0) & (where[-1] < blk_cl), where[-1], blk_cl)
        wide = jnp.concatenate([tiles[row, k] for k in range(nbr_k)], axis=1)
        acc_ref[row] = dot(wide, jnp.concatenate([table[slot] for slot in where], axis=0))


def near_sum(after, nbr, feat, adj, w, t, n_clus, most, room):
    _, blk_cl, block, width = feat.shape
    nbr_k = adj.shape[2]
    pieces = 4 if blk_cl % 4 == 0 else 1
    vmem = pl.BlockSpec(memory_space=pltpu.VMEM)
    smem = pl.BlockSpec(memory_space=pltpu.SMEM)
    hbm = pl.BlockSpec(memory_space=pltpu.HBM)
    return pl.pallas_call(
        functools.partial(near_kernel, t, n_clus, most),
        out_shape=[
            pltpu.VMEM((blk_cl, block, width), F32),
            pltpu.VMEM((blk_cl, block, width), BF16),
            pltpu.VMEM((blk_cl, nbr_k, block, block), BF16),
            jax.ShapeDtypeStruct((blk_cl,), jnp.int32),
        ],
        in_specs=[smem, smem, hbm, hbm, vmem],
        out_specs=[vmem, vmem, vmem, smem],
        scratch_shapes=[
            pltpu.VMEM((blk_cl + 1, block, width), BF16),
            pltpu.SemaphoreType.DMA((2, pieces)),
        ],
        compiler_params=pltpu.CompilerParams(vmem_limit_bytes=room << 20),
        cost_estimate=cost(NEAR_US),
        name="near_sum",
    )(after, nbr, feat, adj, w)


def far_kernel(n_snap, parts, slots, acc_ref, own, tiles, w_ref, *refs):
    n_out = n_snap * len(parts)
    remote, outs = refs[: -n_out - 4], refs[-n_out - 4 : -4]
    done_ref, table, held, sems = refs[-4:]
    done_ref[0] = jnp.int32(0)
    my_snap = lax.axis_index("snap") if n_snap > 1 else jnp.int32(0)
    most, block, width = remote[0].shape
    w = w_ref[...]
    for d, ref in enumerate(remote):
        some = dot(ref[...].reshape(most * block, width), w).astype(BF16)
        table[d * most : (d + 1) * most] = some.reshape(most, block, width)
    table[len(remote) * most] = jnp.zeros((block, width), BF16)
    copies = []
    for e, (lo, hi) in enumerate(parts):
        for d in list(range(1, n_snap)) + [0]:
            p = partner(my_snap, d, n_snap)
            for g in range(lo, hi):
                row = g * n_snap + p
                total = acc_ref[row] + dot(tiles[row, tiles.shape[1] - 1], table[slots[row]])
                total = (own[row].astype(F32) + jnp.maximum(total, 0.0)).astype(BF16)
                if d == 0:
                    outs[e * n_snap][g - lo] = total
                else:
                    held[d - 1, g] = total
            if d > 0:
                copies.append(
                    pltpu.make_async_copy(
                        held.at[d - 1, lo:hi], outs[e * n_snap + d], sems.at[e, d - 1]
                    )
                )
                copies[-1].start()
    for copy in copies:
        copy.wait()


def far_sum(near, remote, w, n_snap, parts):
    acc, own, tiles, slots = near
    most, block, width = remote[0].shape
    vmem = pl.BlockSpec(memory_space=pltpu.VMEM)
    hbm = pl.BlockSpec(memory_space=pltpu.HBM)
    shapes = [(hi - lo, block, width) for lo, hi in parts]
    *out, done = pl.pallas_call(
        functools.partial(far_kernel, n_snap, parts),
        out_shape=[
            (pltpu.HBM if d else pltpu.VMEM)(shape, BF16) for shape in shapes for d in range(n_snap)
        ]
        + [jax.ShapeDtypeStruct((1,), jnp.int32)],
        in_specs=[pl.BlockSpec(memory_space=pltpu.SMEM)] + [vmem] * (4 + len(remote)),
        out_specs=[hbm if d else vmem for _ in shapes for d in range(n_snap)]
        + [pl.BlockSpec(memory_space=pltpu.SMEM)],
        scratch_shapes=[
            pltpu.VMEM((len(remote) * most + 1, block, width), BF16),
            pltpu.VMEM((max(n_snap - 1, 1), parts[-1][1], block, width), BF16),
            pltpu.SemaphoreType.DMA((len(parts), max(n_snap - 1, 1))),
        ],
        compiler_params=pltpu.CompilerParams(vmem_limit_bytes=8 << 20),
        cost_estimate=cost(FAR_US),
        name="far_sum",
    )(slots, acc, own, tiles, w, *remote)
    return [out[e * n_snap : (e + 1) * n_snap] for e in range(len(parts))], done


def prepare_kernel(after_ref, pos_ref, wq_ref, wk_ref, wv_ref, wo_ref, pos, wqkv, wo):
    width = wo.shape[0]
    head_dim = width // HEADS
    to = lax.broadcasted_iota(jnp.int32, (width, width), 0)
    source = lax.broadcasted_iota(jnp.int32, (width, width), 1)
    named = (to & (HEADS - 1)) * head_dim + jnp.right_shift(to, HEADS.bit_length() - 1)
    order = jnp.where(source == named, 1.0, 0.0).astype(BF16)
    for i, ref in enumerate((wq_ref, wk_ref, wv_ref)):
        turned = lax.dot_general(
            order, ref[...], (((1,), (1,)), ((), ())), preferred_element_type=F32
        )
        wqkv[i * width : (i + 1) * width] = turned.astype(BF16)
    wo[...] = dot(order, wo_ref[...]).astype(BF16)
    pos[...] = pos_ref[...].astype(F32)


def prepare(after, pos, wq, wk, wv, wo):
    width = wo.shape[0]
    vmem = pl.BlockSpec(memory_space=pltpu.VMEM)
    return pl.pallas_call(
        prepare_kernel,
        out_shape=[
            pltpu.VMEM(pos.shape, F32),
            pltpu.VMEM((3 * width, width), BF16),
            pltpu.VMEM((width, width), BF16),
        ],
        in_specs=[pl.BlockSpec(memory_space=pltpu.SMEM)] + [vmem] * 5,
        out_specs=[vmem] * 3,
        compiler_params=pltpu.CompilerParams(vmem_limit_bytes=4 << 20),
        cost_estimate=cost(1),
        name="prepare",
    )(after, pos, wq, wk, wv, wo)


def temporal_kernel(n_snap, per, blocks, chunk, *refs):
    count = n_snap * per
    ins = refs[:count]
    pos_ref, wqkv_ref, wo_ref, wup_ref, bias_ref, wdown_ref = refs[count : count + 6]
    outs = refs[-5 - n_snap : -5]
    raw, zs, qkv, att, out_sems = refs[-5:]
    me = lax.axis_index("snap")
    nsnap, nvert, width = zs.shape
    head_dim = width // HEADS
    for d in range(n_snap):
        for j in range(per):
            i = d * per + j
            raw[came_from(me, d, n_snap) * per + j] = ins[i][blocks[i]]

    for t in range(nsnap):
        zs[t] = (raw[t].astype(F32) + pos_ref[t : t + 1, :]).astype(BF16)
        qkv[t] = (
            lax.dot_general(
                wqkv_ref[...], zs[t], (((1,), (1,)), ((), ())), preferred_element_type=F32
            )
            .astype(BF16)
            .astype(F32)
        )

    def part(which, t):
        return qkv[t, which * width : (which + 1) * width, :].reshape(head_dim, HEADS, nvert)

    for t in range(nsnap):
        q = part(0, t)
        scores = [
            jnp.sum(q * part(1, s), axis=0) * (1.0 / math.sqrt(head_dim)) for s in range(t + 1)
        ]
        peak = functools.reduce(jnp.maximum, scores)
        expo = [jnp.exp(x - peak) for x in scores]
        total = functools.reduce(jnp.add, expo)
        acc = None
        for s in range(t + 1):
            prob = (expo[s] / total).astype(BF16).astype(F32)
            term = prob[None] * part(2, s)
            acc = term if acc is None else acc + term
        att[t] = acc.reshape(width, nvert).astype(BF16)

    def send(d, first):
        target = outs[d]
        if d == 0:
            target = target.at[:, pl.ds((chunk * n_snap + me) * nvert, nvert)]
        return pltpu.make_async_copy(raw.at[pl.ds(first, per)], target, out_sems.at[d])

    for g in range(n_snap):
        some = slice(g * per, (g + 1) * per)
        z = zs[some].reshape(per * nvert, width)
        joined = jnp.concatenate([att[g * per + j] for j in range(per)], axis=1)
        mixed = z.astype(F32) + lax.dot_general(
            joined, wo_ref[...], (((0,), (0,)), ((), ())), preferred_element_type=F32
        )
        hidden = jnp.maximum(dot(mixed.astype(BF16), wup_ref[...]) + bias_ref[...], 0.0)
        out = mixed + dot(hidden.astype(BF16), wdown_ref[...])
        raw[some] = out.astype(BF16).reshape(per, nvert, width)
        for d in range(n_snap):

            @pl.when(partner(me, d, n_snap) == g)
            def _():
                send(d, g * per).start()

    for d in range(n_snap):
        send(d, partner(me, d, n_snap) * per).wait()


def temporal_chunk(ins, blocks, weights, n_snap, per, chunk, chunks, result, waits):
    _, block, width = ins[0].shape
    nsnap = n_snap * per
    vmem = pl.BlockSpec(memory_space=pltpu.VMEM)
    hbm = pl.BlockSpec(memory_space=pltpu.HBM)
    before = [] if result is None else [result]
    n_in = len(ins) + len(weights)
    return pl.pallas_call(
        functools.partial(temporal_kernel, n_snap, per, blocks, chunk),
        out_shape=[pltpu.HBM((per, chunks * n_snap * block, width), BF16)]
        + [pltpu.HBM((per, block, width), BF16)] * (n_snap - 1),
        in_specs=[vmem] * (len(ins) + len(weights)) + [hbm] * len(before)
        + [pl.BlockSpec(memory_space=pltpu.SMEM)] * len(waits),
        out_specs=[hbm] * n_snap,
        input_output_aliases={n_in: 0} if before else {},
        scratch_shapes=[
            pltpu.VMEM((nsnap, block, width), BF16),
            pltpu.VMEM((nsnap, block, width), BF16),
            pltpu.VMEM((nsnap, 3 * width, block), F32),
            pltpu.VMEM((nsnap, width, block), BF16),
            pltpu.SemaphoreType.DMA((n_snap,)),
        ],
        compiler_params=pltpu.CompilerParams(vmem_limit_bytes=14 << 20),
        cost_estimate=cost(TEMPORAL_US),
        name="temporal_chunk",
    )(*ins, *weights, *before, *waits)


def place_kernel(n_snap, chunk, *refs):
    blocks, (_, out_ref, sems) = refs[: n_snap - 1], refs[n_snap - 1 :]
    block = blocks[0].shape[1]
    me = lax.axis_index("snap")
    copies = []
    for d in range(1, n_snap):
        row = (chunk * n_snap + came_from(me, d, n_snap)) * block
        copies.append(
            pltpu.make_async_copy(blocks[d - 1], out_ref.at[:, pl.ds(row, block)], sems.at[d - 1])
        )
        copies[-1].start()
    for copy in copies:
        copy.wait()


def place(result, blocks, n_snap, chunk):
    hbm = pl.BlockSpec(memory_space=pltpu.HBM)
    return pl.pallas_call(
        functools.partial(place_kernel, n_snap, chunk),
        out_shape=pltpu.HBM(result.shape, result.dtype),
        in_specs=[pl.BlockSpec(memory_space=pltpu.VMEM)] * len(blocks) + [hbm],
        out_specs=hbm,
        input_output_aliases={len(blocks): 0},
        scratch_shapes=[pltpu.SemaphoreType.DMA((n_snap - 1,))],
        compiler_params=pltpu.CompilerParams(vmem_limit_bytes=1 << 20),
        cost_estimate=cost(PLACE_US),
        name="place",
    )(*blocks, result)


def shift(x, d, n):
    return lax.ppermute(x, "snap", [(i, partner(i, d, n)) for i in range(n)])


def temporal_fast(got, parts, weights, n_snap, first):
    per = len(got)
    chunks = parts[0][-1][1]
    result, backs = None, []
    for c in range(chunks):
        ins, blocks = [], []
        for d in range(n_snap):
            for j in range(per):
                e = [lo <= c < hi for lo, hi in parts[j]].index(True)
                ins.append(got[j][e][d])
                blocks.append(c - parts[j][e][0])
        result, *sent = temporal_chunk(
            ins, blocks, weights, n_snap, per, c, chunks, result, first if c == 0 else []
        )
        backs.append([shift(x, d + 1, n_snap) for d, x in enumerate(sent)])
        if c >= LAG:
            result = place(result, backs[c - LAG], n_snap, c - LAG)
    for c in range(max(chunks - LAG, 0), chunks):
        result = place(result, backs[c], n_snap, c)
    return result


def temporal_plain(zvals, w_query, w_key, w_value, w_out, w_up, up_bias, w_down):
    nsnap, nvert, width = zvals.shape
    head_dim = width // HEADS
    heads = (nsnap, nvert, HEADS, head_dim)
    q_heads = dot(zvals, w_query).astype(BF16).reshape(heads)
    k_heads = dot(zvals, w_key).astype(BF16).reshape(heads)
    v_heads = dot(zvals, w_value).astype(BF16).reshape(heads)
    scores = jnp.einsum("tvhd,svhd->vhts", q_heads, k_heads, preferred_element_type=F32)
    scores = scores * (1.0 / math.sqrt(head_dim))
    causal = jnp.arange(nsnap)[:, None] >= jnp.arange(nsnap)[None, :]
    scores = jnp.where(causal, scores, NEG)
    peak = jnp.max(scores, axis=-1, keepdims=True)
    expo = jnp.exp(scores - peak)
    probs = (expo / jnp.sum(expo, axis=-1, keepdims=True)).astype(BF16)
    attended = jnp.einsum("vhts,svhd->tvhd", probs, v_heads, preferred_element_type=F32)
    attended = attended.astype(BF16).reshape(nsnap, nvert, width)
    mixed = zvals.astype(F32) + dot(attended, w_out)
    hidden = jax.nn.relu(dot(mixed.astype(BF16), w_up) + up_bias).astype(BF16)
    return (mixed + dot(hidden, w_down)).astype(BF16)


def on_device(
    features,
    adj_tiles,
    neighbors,
    w_struct,
    pos_embed,
    w_query,
    w_key,
    w_value,
    w_out,
    w_up,
    up_bias,
    w_down,
):
    snap_dev, vert_cl, width = features.shape
    blk_cl, nbr_k, block = adj_tiles.shape[1:4]
    n_clus, n_snap = lax.axis_size("clus"), lax.axis_size("snap")
    most = 4
    nbr = neighbors.transpose(0, 2, 1)
    feat = features.reshape(snap_dev, blk_cl, block, width)
    fast = snap_dev * n_snap <= 8 and blk_cl % n_snap == 0 and block % LANES == 0
    groups = n_snap if fast else 1
    chunks = blk_cl // groups
    done = jnp.zeros((1,), jnp.int32)
    sets = []
    for t in range(snap_dev):
        some, done = gather_blocks(done, nbr, feat, t, most, n_clus)
        sets.append(some)
    got, parts, prepared = [], [], None
    for t in range(snap_dev):
        near = near_sum(done, nbr, feat, adj_tiles, w_struct, t, n_clus, most, ROOM[min(t, 1)])
        if t == 0:
            for later in range(1, snap_dev):
                sets[later], _ = gate(near[:1], sets[later])
        remote = [
            lax.ppermute(x, "clus", [(i, partner(i, d + 1, n_clus)) for i in range(n_clus)])
            for d, x in enumerate(sets[t])
        ]
        last = t == snap_dev - 1 and fast and chunks > 1
        parts.append([(0, 1), (1, chunks)] if last else [(0, chunks)])
        sent, done = far_sum(near, remote, w_struct, groups, parts[-1])
        got.append([])
        for e, part in enumerate(sent):
            if t > 0 and n_snap > 2:
                waits = got[-2][-1][1:2] if e == 0 else got[-2][-1][2:3] + got[-1][-1][1:2]
                part[1:], done = gate(waits, part[1:])
            got[-1].append([x if d == 0 else shift(x, d, n_snap) for d, x in enumerate(part)])
        if t == 0 and fast:
            prepared = prepare(done, pos_embed, w_query, w_key, w_value, w_out)
    if fast:
        weights = (*prepared, w_up, up_bias.reshape(1, -1), w_down)
        return temporal_fast(got, parts, weights, n_snap, [done])
    vert_dev = vert_cl // n_snap
    struct_out = jnp.stack([g[0][0].reshape(n_snap, vert_dev, width) for g in got])
    inputs = lax.all_to_all(struct_out, "snap", split_axis=1, concat_axis=0, tiled=True)[:, 0]
    zvals = (inputs.astype(F32) + pos_embed.astype(F32)[:, None, :]).astype(BF16)
    result = temporal_plain(zvals, w_query, w_key, w_value, w_out, w_up, up_bias, w_down)
    returned = lax.all_to_all(
        result[:, None], "snap", split_axis=0, concat_axis=1, tiled=True
    )
    return returned.reshape(snap_dev, vert_cl, width)


def solution(mesh):
    placed = (
        P(("grp", "snap"), "clus", None),
        P(("grp", "snap"), "clus", None, None, None),
        P(("grp", "snap"), None, None),
        P(),
        P(),
        P(),
        P(),
        P(),
        P(),
        P(),
        P(),
        P(),
    )
    return jax.shard_map(
        on_device,
        mesh=mesh,
        in_specs=placed,
        out_specs=P(("grp", "snap"), "clus", None),
        check_vma=False,
    )
```

```python
import functools
import math

import jax
import jax.numpy as jnp
from jax import lax
from jax.experimental import pallas as pl
from jax.experimental.pallas import tpu as pltpu
from jax.sharding import PartitionSpec as P

HEADS = 8
LANES = 128
LAG = 2
ALONE, ROOM = 60, (57, 46)
GATHER_US, GATE_US, NEAR_US, FAR_US, TEMPORAL_US, PLACE_US = 3, 0.5, 3, 2, 3, 1
NEG = -1e30
F32 = jnp.float32
BF16 = jnp.bfloat16


def cost(us):
    return pl.CostEstimate(flops=0, bytes_accessed=int(us * 3.0e4), transcendentals=0)


def dot(a, b):
    return jnp.dot(a, b, preferred_element_type=F32)


def partner(me, d, n):
    return me ^ d if n & (n - 1) == 0 else (me + d) % n


def came_from(me, d, n):
    return me ^ d if n & (n - 1) == 0 else (me + n - d) % n


def named_mask(nbr_ref, t, first, cluster, blk_cl):
    last = nbr_ref.shape[1] - 1
    base = cluster * blk_cl
    mask = jnp.int32(0)
    for i in range(blk_cl):
        g = nbr_ref[t, last, first + i] - base
        mask |= jnp.where((g >= 0) & (g < blk_cl), jnp.left_shift(1, g & 31), 0)
    return mask


def lowest_bit(mask, blk_cl):
    low = mask & -mask
    place = jnp.int32(0)
    for i in range((blk_cl - 1).bit_length()):
        holes = sum(1 << b for b in range(blk_cl) if b >> i & 1)
        place += jnp.where((low & holes) != 0, 1 << i, 0)
    return place


def gather_kernel(t, most, n_clus, direct, after_ref, nbr_ref, feat_ref, *refs):
    blk_cl = feat_ref.shape[1]
    outs, (done_ref, held, in_sems, out_sems) = refs[: n_clus - 1], refs[n_clus - 1 :]
    done_ref[0] = jnp.int32(0)
    me = lax.axis_index("clus")
    arrivals, copies = {}, []
    order = list(range(n_clus - 1, 0, -1))
    for d in order:
        mask = named_mask(nbr_ref, t, partner(me, d, n_clus) * blk_cl, me, blk_cl)
        picked = []
        for _ in range(most):
            picked.append(lowest_bit(mask, blk_cl))
            mask &= mask - 1
        target = outs[d - 1] if direct else held.at[d - 1]
        arrivals[d] = [
            pltpu.make_async_copy(feat_ref.at[t, picked[j]], target.at[j], in_sems.at[d - 1, j])
            for j in range(most)
        ]
        for copy in arrivals[d]:
            copy.start()
    for d in order:
        for copy in arrivals[d]:
            copy.wait()
        if not direct:
            copies.append(pltpu.make_async_copy(held.at[d - 1], outs[d - 1], out_sems.at[d - 1]))
            copies[-1].start()
    for copy in copies:
        copy.wait()


def gather_blocks(after, nbr, feat, t, most, n_clus):
    direct = t == 0
    _, _, block, width = feat.shape
    shape = (most, block, width)
    smem = pl.BlockSpec(memory_space=pltpu.SMEM)
    space = pltpu.VMEM if direct else pltpu.HBM
    *out, done = pl.pallas_call(
        functools.partial(gather_kernel, t, most, n_clus, direct),
        out_shape=[space(shape, BF16)] * (n_clus - 1) + [jax.ShapeDtypeStruct((1,), jnp.int32)],
        in_specs=[smem, smem, pl.BlockSpec(memory_space=pltpu.HBM)],
        out_specs=[pl.BlockSpec(memory_space=space)] * (n_clus - 1) + [smem],
        scratch_shapes=[
            pltpu.VMEM((n_clus - 1,) + (shape if not direct else (1, 16, 128)), BF16),
            pltpu.SemaphoreType.DMA((n_clus - 1, most)),
            pltpu.SemaphoreType.DMA((n_clus - 1,)),
        ],
        compiler_params=pltpu.CompilerParams(vmem_limit_bytes=ALONE << 20),
        cost_estimate=cost(GATHER_US),
        name="gather_blocks",
    )(after, nbr, feat)
    return out, done


def gate_kernel(*refs):
    refs[-1][0] = jnp.int32(0)


def gate(after, xs):
    hbm = pl.BlockSpec(memory_space=pltpu.HBM)
    *out, done = pl.pallas_call(
        gate_kernel,
        out_shape=[pltpu.HBM(x.shape, x.dtype) for x in xs]
        + [jax.ShapeDtypeStruct((1,), jnp.int32)],
        in_specs=[pl.BlockSpec(memory_space=pl.ANY)] * len(after) + [hbm] * len(xs),
        out_specs=[hbm] * len(xs) + [pl.BlockSpec(memory_space=pltpu.SMEM)],
        input_output_aliases={i + len(after): i for i in range(len(xs))},
        compiler_params=pltpu.CompilerParams(vmem_limit_bytes=1 << 20),
        cost_estimate=cost(GATE_US),
        name="gate",
    )(*after, *xs)
    return out, done


def near_kernel(
    t, n_clus, most, after_ref, nbr_ref, feat_ref, adj_ref, w_ref, acc_ref, own, tiles, slots, table, sems
):
    my_clus = lax.axis_index("clus")
    blk_cl, block, width = own.shape
    nbr_k = tiles.shape[1]
    pieces = sems.shape[1]
    rows = blk_cl // pieces
    first = my_clus * blk_cl
    copies = []
    for source, target in ((feat_ref, own), (adj_ref, tiles)):
        for i in range(pieces):
            some = pl.ds(i * rows, rows)
            copies.append(
                pltpu.make_async_copy(
                    source.at[t, some], target.at[some], sems.at[len(copies) // pieces, i]
                )
            )
            copies[-1].start()
    for i in range(blk_cl):
        slots[i] = (n_clus - 1) * most
    for d in range(1, n_clus):
        other = came_from(my_clus, d, n_clus)
        mask = named_mask(nbr_ref, t, first, other, blk_cl)
        for i in range(blk_cl):
            b = nbr_ref[t, nbr_k - 1, first + i] - other * blk_cl
            below = mask & (jnp.left_shift(1, b & 31) - 1)
            rank = jnp.int32(0)
            for _ in range(most):
                rank += jnp.where(below != 0, 1, 0)
                below &= below - 1
            slots[i] = jnp.where((b >= 0) & (b < blk_cl), (d - 1) * most + rank, slots[i])
    w = w_ref[...]
    for i in range(pieces):
        copies[i].wait()
        some = own[i * rows : (i + 1) * rows].reshape(rows * block, width)
        table[i * rows : (i + 1) * rows] = dot(some, w).astype(BF16).reshape(rows, block, width)
    table[blk_cl] = jnp.zeros((block, width), BF16)
    for row in range(blk_cl):
        if row % rows == 0:
            copies[pieces + row // rows].wait()
        where = [nbr_ref[t, k, first + row] - first for k in range(nbr_k)]
        where[-1] = jnp.where((where[-1] >= 0) & (where[-1] < blk_cl), where[-1], blk_cl)
        wide = jnp.concatenate([tiles[row, k] for k in range(nbr_k)], axis=1)
        acc_ref[row] = dot(wide, jnp.concatenate([table[slot] for slot in where], axis=0))


def near_sum(after, nbr, feat, adj, w, t, n_clus, most, room):
    _, blk_cl, block, width = feat.shape
    nbr_k = adj.shape[2]
    pieces = 4 if blk_cl % 4 == 0 else 1
    vmem = pl.BlockSpec(memory_space=pltpu.VMEM)
    smem = pl.BlockSpec(memory_space=pltpu.SMEM)
    hbm = pl.BlockSpec(memory_space=pltpu.HBM)
    return pl.pallas_call(
        functools.partial(near_kernel, t, n_clus, most),
        out_shape=[
            pltpu.VMEM((blk_cl, block, width), F32),
            pltpu.VMEM((blk_cl, block, width), BF16),
            pltpu.VMEM((blk_cl, nbr_k, block, block), BF16),
            jax.ShapeDtypeStruct((blk_cl,), jnp.int32),
        ],
        in_specs=[smem, smem, hbm, hbm, vmem],
        out_specs=[vmem, vmem, vmem, smem],
        scratch_shapes=[
            pltpu.VMEM((blk_cl + 1, block, width), BF16),
            pltpu.SemaphoreType.DMA((2, pieces)),
        ],
        compiler_params=pltpu.CompilerParams(vmem_limit_bytes=room << 20),
        cost_estimate=cost(NEAR_US),
        name="near_sum",
    )(after, nbr, feat, adj, w)


def far_kernel(n_snap, parts, direct, slots, acc_ref, own, tiles, w_ref, *refs):
    n_out = n_snap * len(parts)
    remote, outs = refs[: -n_out - 4], refs[-n_out - 4 : -4]
    done_ref, table, held, sems = refs[-4:]
    done_ref[0] = jnp.int32(0)
    my_snap = lax.axis_index("snap") if n_snap > 1 else jnp.int32(0)
    most, block, width = remote[0].shape
    w = w_ref[...]
    for d, ref in enumerate(remote):
        some = dot(ref[...].reshape(most * block, width), w).astype(BF16)
        table[d * most : (d + 1) * most] = some.reshape(most, block, width)
    table[len(remote) * most] = jnp.zeros((block, width), BF16)
    copies = []
    for e, (lo, hi) in enumerate(parts):
        for d in list(range(1, n_snap)) + [0]:
            p = partner(my_snap, d, n_snap)
            for g in range(lo, hi):
                row = g * n_snap + p
                total = acc_ref[row] + dot(tiles[row, tiles.shape[1] - 1], table[slots[row]])
                total = (own[row].astype(F32) + jnp.maximum(total, 0.0)).astype(BF16)
                if d == 0 or direct:
                    outs[e * n_snap + d][g - lo] = total
                else:
                    held[d - 1, g] = total
            if d > 0 and not direct:
                copies.append(
                    pltpu.make_async_copy(
                        held.at[d - 1, lo:hi], outs[e * n_snap + d], sems.at[e, d - 1]
                    )
                )
                copies[-1].start()
    for copy in copies:
        copy.wait()


def far_sum(near, remote, w, n_snap, parts, direct):
    acc, own, tiles, slots = near
    most, block, width = remote[0].shape
    vmem = pl.BlockSpec(memory_space=pltpu.VMEM)
    hbm = pl.BlockSpec(memory_space=pltpu.HBM)
    shapes = [(hi - lo, block, width) for lo, hi in parts]
    *out, done = pl.pallas_call(
        functools.partial(far_kernel, n_snap, parts, direct),
        out_shape=[
            (pltpu.VMEM if d == 0 or direct else pltpu.HBM)(shape, BF16) for shape in shapes for d in range(n_snap)
        ]
        + [jax.ShapeDtypeStruct((1,), jnp.int32)],
        in_specs=[pl.BlockSpec(memory_space=pltpu.SMEM)] + [vmem] * (4 + len(remote)),
        out_specs=[vmem if d == 0 or direct else hbm for _ in shapes for d in range(n_snap)]
        + [pl.BlockSpec(memory_space=pltpu.SMEM)],
        scratch_shapes=[
            pltpu.VMEM((len(remote) * most + 1, block, width), BF16),
            pltpu.VMEM((max(n_snap - 1, 1), parts[-1][1], block, width), BF16),
            pltpu.SemaphoreType.DMA((len(parts), max(n_snap - 1, 1))),
        ],
        compiler_params=pltpu.CompilerParams(vmem_limit_bytes=8 << 20),
        cost_estimate=cost(FAR_US),
        name="far_sum",
    )(slots, acc, own, tiles, w, *remote)
    return [out[e * n_snap : (e + 1) * n_snap] for e in range(len(parts))], done


def prepare_kernel(after_ref, pos_ref, wq_ref, wk_ref, wv_ref, wo_ref, pos, wqkv, wo):
    width = wo.shape[0]
    head_dim = width // HEADS
    to = lax.broadcasted_iota(jnp.int32, (width, width), 0)
    source = lax.broadcasted_iota(jnp.int32, (width, width), 1)
    named = (to & (HEADS - 1)) * head_dim + jnp.right_shift(to, HEADS.bit_length() - 1)
    order = jnp.where(source == named, 1.0, 0.0).astype(BF16)
    for i, ref in enumerate((wq_ref, wk_ref, wv_ref)):
        turned = lax.dot_general(
            order, ref[...], (((1,), (1,)), ((), ())), preferred_element_type=F32
        )
        wqkv[i * width : (i + 1) * width] = turned.astype(BF16)
    wo[...] = dot(order, wo_ref[...]).astype(BF16)
    pos[...] = pos_ref[...].astype(F32)


def prepare(after, pos, wq, wk, wv, wo):
    width = wo.shape[0]
    vmem = pl.BlockSpec(memory_space=pltpu.VMEM)
    return pl.pallas_call(
        prepare_kernel,
        out_shape=[
            pltpu.VMEM(pos.shape, F32),
            pltpu.VMEM((3 * width, width), BF16),
            pltpu.VMEM((width, width), BF16),
        ],
        in_specs=[pl.BlockSpec(memory_space=pltpu.SMEM)] + [vmem] * 5,
        out_specs=[vmem] * 3,
        compiler_params=pltpu.CompilerParams(vmem_limit_bytes=4 << 20),
        cost_estimate=cost(1),
        name="prepare",
    )(after, pos, wq, wk, wv, wo)


def temporal_kernel(n_snap, per, blocks, chunk, *refs):
    count = n_snap * per
    ins = refs[:count]
    pos_ref, wqkv_ref, wo_ref, wup_ref, bias_ref, wdown_ref = refs[count : count + 6]
    outs = refs[-5 - n_snap : -5]
    raw, zs, qkv, att, out_sems = refs[-5:]
    me = lax.axis_index("snap")
    nsnap, nvert, width = zs.shape
    head_dim = width // HEADS
    for d in range(n_snap):
        for j in range(per):
            i = d * per + j
            raw[came_from(me, d, n_snap) * per + j] = ins[i][blocks[i]]

    for t in range(nsnap):
        zs[t] = (raw[t].astype(F32) + pos_ref[t : t + 1, :]).astype(BF16)
        qkv[t] = (
            lax.dot_general(
                wqkv_ref[...], zs[t], (((1,), (1,)), ((), ())), preferred_element_type=F32
            )
            .astype(BF16)
            .astype(F32)
        )

    def part(which, t):
        return qkv[t, which * width : (which + 1) * width, :].reshape(head_dim, HEADS, nvert)

    for t in range(nsnap):
        q = part(0, t)
        scores = [
            jnp.sum(q * part(1, s), axis=0) * (1.0 / math.sqrt(head_dim)) for s in range(t + 1)
        ]
        peak = functools.reduce(jnp.maximum, scores)
        expo = [jnp.exp(x - peak) for x in scores]
        total = functools.reduce(jnp.add, expo)
        acc = None
        for s in range(t + 1):
            prob = (expo[s] / total).astype(BF16).astype(F32)
            term = prob[None] * part(2, s)
            acc = term if acc is None else acc + term
        att[t] = acc.reshape(width, nvert).astype(BF16)

    def send(d, first):
        target = outs[d]
        if d == 0:
            target = target.at[:, pl.ds((chunk * n_snap + me) * nvert, nvert)]
        return pltpu.make_async_copy(raw.at[pl.ds(first, per)], target, out_sems.at[d])

    for g in range(n_snap):
        some = slice(g * per, (g + 1) * per)
        z = zs[some].reshape(per * nvert, width)
        joined = jnp.concatenate([att[g * per + j] for j in range(per)], axis=1)
        mixed = z.astype(F32) + lax.dot_general(
            joined, wo_ref[...], (((0,), (0,)), ((), ())), preferred_element_type=F32
        )
        hidden = jnp.maximum(dot(mixed.astype(BF16), wup_ref[...]) + bias_ref[...], 0.0)
        out = mixed + dot(hidden.astype(BF16), wdown_ref[...])
        raw[some] = out.astype(BF16).reshape(per, nvert, width)
        for d in range(n_snap):

            @pl.when(partner(me, d, n_snap) == g)
            def _():
                send(d, g * per).start()

    for d in range(n_snap):
        send(d, partner(me, d, n_snap) * per).wait()


def temporal_chunk(ins, blocks, weights, n_snap, per, chunk, chunks, result, waits):
    _, block, width = ins[0].shape
    nsnap = n_snap * per
    vmem = pl.BlockSpec(memory_space=pltpu.VMEM)
    hbm = pl.BlockSpec(memory_space=pltpu.HBM)
    before = [] if result is None else [result]
    n_in = len(ins) + len(weights)
    return pl.pallas_call(
        functools.partial(temporal_kernel, n_snap, per, blocks, chunk),
        out_shape=[pltpu.HBM((per, chunks * n_snap * block, width), BF16)]
        + [pltpu.HBM((per, block, width), BF16)] * (n_snap - 1),
        in_specs=[vmem] * (len(ins) + len(weights)) + [hbm] * len(before)
        + [pl.BlockSpec(memory_space=pltpu.SMEM)] * len(waits),
        out_specs=[hbm] * n_snap,
        input_output_aliases={n_in: 0} if before else {},
        scratch_shapes=[
            pltpu.VMEM((nsnap, block, width), BF16),
            pltpu.VMEM((nsnap, block, width), BF16),
            pltpu.VMEM((nsnap, 3 * width, block), F32),
            pltpu.VMEM((nsnap, width, block), BF16),
            pltpu.SemaphoreType.DMA((n_snap,)),
        ],
        compiler_params=pltpu.CompilerParams(vmem_limit_bytes=14 << 20),
        cost_estimate=cost(TEMPORAL_US),
        name="temporal_chunk",
    )(*ins, *weights, *before, *waits)


def place_kernel(n_snap, chunk, *refs):
    blocks, (_, out_ref, sems) = refs[: n_snap - 1], refs[n_snap - 1 :]
    block = blocks[0].shape[1]
    me = lax.axis_index("snap")
    copies = []
    for d in range(1, n_snap):
        row = (chunk * n_snap + came_from(me, d, n_snap)) * block
        copies.append(
            pltpu.make_async_copy(blocks[d - 1], out_ref.at[:, pl.ds(row, block)], sems.at[d - 1])
        )
        copies[-1].start()
    for copy in copies:
        copy.wait()


def place(result, blocks, n_snap, chunk):
    hbm = pl.BlockSpec(memory_space=pltpu.HBM)
    return pl.pallas_call(
        functools.partial(place_kernel, n_snap, chunk),
        out_shape=pltpu.HBM(result.shape, result.dtype),
        in_specs=[pl.BlockSpec(memory_space=pltpu.VMEM)] * len(blocks) + [hbm],
        out_specs=hbm,
        input_output_aliases={len(blocks): 0},
        scratch_shapes=[pltpu.SemaphoreType.DMA((n_snap - 1,))],
        compiler_params=pltpu.CompilerParams(vmem_limit_bytes=1 << 20),
        cost_estimate=cost(PLACE_US),
        name="place",
    )(*blocks, result)


def shift(x, d, n):
    return lax.ppermute(x, "snap", [(i, partner(i, d, n)) for i in range(n)])


def temporal_fast(got, parts, weights, n_snap, first):
    per = len(got)
    chunks = parts[0][-1][1]
    result, backs = None, []
    for c in range(chunks):
        ins, blocks = [], []
        for d in range(n_snap):
            for j in range(per):
                e = [lo <= c < hi for lo, hi in parts[j]].index(True)
                ins.append(got[j][e][d])
                blocks.append(c - parts[j][e][0])
        result, *sent = temporal_chunk(
            ins, blocks, weights, n_snap, per, c, chunks, result, first if c == 0 else []
        )
        backs.append([shift(x, d + 1, n_snap) for d, x in enumerate(sent)])
        if c >= LAG:
            result = place(result, backs[c - LAG], n_snap, c - LAG)
    for c in range(max(chunks - LAG, 0), chunks):
        result = place(result, backs[c], n_snap, c)
    return result


def temporal_plain(zvals, w_query, w_key, w_value, w_out, w_up, up_bias, w_down):
    nsnap, nvert, width = zvals.shape
    head_dim = width // HEADS
    heads = (nsnap, nvert, HEADS, head_dim)
    q_heads = dot(zvals, w_query).astype(BF16).reshape(heads)
    k_heads = dot(zvals, w_key).astype(BF16).reshape(heads)
    v_heads = dot(zvals, w_value).astype(BF16).reshape(heads)
    scores = jnp.einsum("tvhd,svhd->vhts", q_heads, k_heads, preferred_element_type=F32)
    scores = scores * (1.0 / math.sqrt(head_dim))
    causal = jnp.arange(nsnap)[:, None] >= jnp.arange(nsnap)[None, :]
    scores = jnp.where(causal, scores, NEG)
    peak = jnp.max(scores, axis=-1, keepdims=True)
    expo = jnp.exp(scores - peak)
    probs = (expo / jnp.sum(expo, axis=-1, keepdims=True)).astype(BF16)
    attended = jnp.einsum("vhts,svhd->tvhd", probs, v_heads, preferred_element_type=F32)
    attended = attended.astype(BF16).reshape(nsnap, nvert, width)
    mixed = zvals.astype(F32) + dot(attended, w_out)
    hidden = jax.nn.relu(dot(mixed.astype(BF16), w_up) + up_bias).astype(BF16)
    return (mixed + dot(hidden, w_down)).astype(BF16)


def on_device(
    features,
    adj_tiles,
    neighbors,
    w_struct,
    pos_embed,
    w_query,
    w_key,
    w_value,
    w_out,
    w_up,
    up_bias,
    w_down,
):
    snap_dev, vert_cl, width = features.shape
    blk_cl, nbr_k, block = adj_tiles.shape[1:4]
    n_clus, n_snap = lax.axis_size("clus"), lax.axis_size("snap")
    most = 4
    nbr = neighbors.transpose(0, 2, 1)
    feat = features.reshape(snap_dev, blk_cl, block, width)
    fast = snap_dev * n_snap <= 8 and blk_cl % n_snap == 0 and block % LANES == 0
    groups = n_snap if fast else 1
    chunks = blk_cl // groups
    done = jnp.zeros((1,), jnp.int32)
    sets = []
    for t in range(snap_dev):
        some, done = gather_blocks(done, nbr, feat, t, most, n_clus)
        sets.append(some)
    got, parts, prepared = [], [], None
    for t in range(snap_dev):
        near = near_sum(done, nbr, feat, adj_tiles, w_struct, t, n_clus, most, ROOM[min(t, 1)])
        if t == 0:
            for later in range(1, snap_dev):
                sets[later], _ = gate(near[:1], sets[later])
        remote = {}
        for d in range(n_clus - 1, 0, -1):
            pairs = [(i, partner(i, d, n_clus)) for i in range(n_clus)]
            remote[d] = lax.ppermute(sets[t][d - 1], "clus", pairs)
        remote = [remote[d] for d in range(1, n_clus)]
        last = t == snap_dev - 1 and fast and chunks > 1
        parts.append([(0, 1), (1, chunks)] if last else [(0, chunks)])
        sent, done = far_sum(near, remote, w_struct, groups, parts[-1], t == 0)
        got.append([])
        for e, part in enumerate(sent):
            if t > 0 and n_snap > 2:
                waits = got[-2][-1][1:2] if e == 0 else got[-2][-1][2:3] + got[-1][-1][1:2]
                part[1:], done = gate(waits, part[1:])
            got[-1].append([x if d == 0 else shift(x, d, n_snap) for d, x in enumerate(part)])
        if t == 0 and fast:
            prepared = prepare(done, pos_embed, w_query, w_key, w_value, w_out)
    if fast:
        weights = (*prepared, w_up, up_bias.reshape(1, -1), w_down)
        return temporal_fast(got, parts, weights, n_snap, [done])
    vert_dev = vert_cl // n_snap
    struct_out = jnp.stack([g[0][0].reshape(n_snap, vert_dev, width) for g in got])
    inputs = lax.all_to_all(struct_out, "snap", split_axis=1, concat_axis=0, tiled=True)[:, 0]
    zvals = (inputs.astype(F32) + pos_embed.astype(F32)[:, None, :]).astype(BF16)
    result = temporal_plain(zvals, w_query, w_key, w_value, w_out, w_up, up_bias, w_down)
    returned = lax.all_to_all(
        result[:, None], "snap", split_axis=0, concat_axis=1, tiled=True
    )
    return returned.reshape(snap_dev, vert_cl, width)


def solution(mesh):
    placed = (
        P(("grp", "snap"), "clus", None),
        P(("grp", "snap"), "clus", None, None, None),
        P(("grp", "snap"), None, None),
        P(),
        P(),
        P(),
        P(),
        P(),
        P(),
        P(),
        P(),
        P(),
    )
    return jax.shard_map(
        on_device,
        mesh=mesh,
        in_specs=placed,
        out_specs=P(("grp", "snap"), "clus", None),
        check_vma=False,
    )
```

```python
import functools
import math

import jax
import jax.numpy as jnp
from jax import lax
from jax.experimental import pallas as pl
from jax.experimental.pallas import tpu as pltpu
from jax.sharding import PartitionSpec as P

HEADS = 8
LANES = 128
LAG = 3
ALONE, ROOM = 60, (57, 46)
GATHER_US, GATE_US, NEAR_US, FAR_US, TEMPORAL_US, PLACE_US = 3, 0.5, 3, 2, 3, 1
NEG = -1e30
F32 = jnp.float32
BF16 = jnp.bfloat16


def cost(us):
    return pl.CostEstimate(flops=0, bytes_accessed=int(us * 3.0e4), transcendentals=0)


def dot(a, b):
    return jnp.dot(a, b, preferred_element_type=F32)


def partner(me, d, n):
    return me ^ d if n & (n - 1) == 0 else (me + d) % n


def came_from(me, d, n):
    return me ^ d if n & (n - 1) == 0 else (me + n - d) % n


def named_mask(nbr_ref, t, first, cluster, blk_cl):
    last = nbr_ref.shape[1] - 1
    base = cluster * blk_cl
    mask = jnp.int32(0)
    for i in range(blk_cl):
        g = nbr_ref[t, last, first + i] - base
        mask |= jnp.where((g >= 0) & (g < blk_cl), jnp.left_shift(1, g & 31), 0)
    return mask


def lowest_bit(mask, blk_cl):
    low = mask & -mask
    place = jnp.int32(0)
    for i in range((blk_cl - 1).bit_length()):
        holes = sum(1 << b for b in range(blk_cl) if b >> i & 1)
        place += jnp.where((low & holes) != 0, 1 << i, 0)
    return place


def gather_kernel(t, most, n_clus, direct, after_ref, nbr_ref, feat_ref, *refs):
    blk_cl = feat_ref.shape[1]
    outs, (done_ref, held, in_sems, out_sems) = refs[: n_clus - 1], refs[n_clus - 1 :]
    done_ref[0] = jnp.int32(0)
    me = lax.axis_index("clus")
    arrivals, copies = {}, []
    order = list(range(n_clus - 1, 0, -1))
    for d in order:
        mask = named_mask(nbr_ref, t, partner(me, d, n_clus) * blk_cl, me, blk_cl)
        picked = []
        for _ in range(most):
            picked.append(lowest_bit(mask, blk_cl))
            mask &= mask - 1
        target = outs[d - 1] if direct else held.at[d - 1]
        arrivals[d] = [
            pltpu.make_async_copy(feat_ref.at[t, picked[j]], target.at[j], in_sems.at[d - 1, j])
            for j in range(most)
        ]
        for copy in arrivals[d]:
            copy.start()
    for d in order:
        for copy in arrivals[d]:
            copy.wait()
        if not direct:
            copies.append(pltpu.make_async_copy(held.at[d - 1], outs[d - 1], out_sems.at[d - 1]))
            copies[-1].start()
    for copy in copies:
        copy.wait()


def gather_blocks(after, nbr, feat, t, most, n_clus):
    direct = t == 0
    _, _, block, width = feat.shape
    shape = (most, block, width)
    smem = pl.BlockSpec(memory_space=pltpu.SMEM)
    space = pltpu.VMEM if direct else pltpu.HBM
    *out, done = pl.pallas_call(
        functools.partial(gather_kernel, t, most, n_clus, direct),
        out_shape=[space(shape, BF16)] * (n_clus - 1) + [jax.ShapeDtypeStruct((1,), jnp.int32)],
        in_specs=[smem, smem, pl.BlockSpec(memory_space=pltpu.HBM)],
        out_specs=[pl.BlockSpec(memory_space=space)] * (n_clus - 1) + [smem],
        scratch_shapes=[
            pltpu.VMEM((n_clus - 1,) + (shape if not direct else (1, 16, 128)), BF16),
            pltpu.SemaphoreType.DMA((n_clus - 1, most)),
            pltpu.SemaphoreType.DMA((n_clus - 1,)),
        ],
        compiler_params=pltpu.CompilerParams(vmem_limit_bytes=ALONE << 20),
        cost_estimate=cost(GATHER_US),
        name="gather_blocks",
    )(after, nbr, feat)
    return out, done


def gate_kernel(*refs):
    refs[-1][0] = jnp.int32(0)


def gate(after, xs):
    hbm = pl.BlockSpec(memory_space=pltpu.HBM)
    *out, done = pl.pallas_call(
        gate_kernel,
        out_shape=[pltpu.HBM(x.shape, x.dtype) for x in xs]
        + [jax.ShapeDtypeStruct((1,), jnp.int32)],
        in_specs=[pl.BlockSpec(memory_space=pl.ANY)] * len(after) + [hbm] * len(xs),
        out_specs=[hbm] * len(xs) + [pl.BlockSpec(memory_space=pltpu.SMEM)],
        input_output_aliases={i + len(after): i for i in range(len(xs))},
        compiler_params=pltpu.CompilerParams(vmem_limit_bytes=1 << 20),
        cost_estimate=cost(GATE_US),
        name="gate",
    )(*after, *xs)
    return out, done


def near_kernel(
    t, n_clus, most, after_ref, nbr_ref, feat_ref, adj_ref, w_ref, acc_ref, own, tiles, slots, table, sems
):
    my_clus = lax.axis_index("clus")
    blk_cl, block, width = own.shape
    nbr_k = tiles.shape[1]
    pieces = sems.shape[1]
    rows = blk_cl // pieces
    first = my_clus * blk_cl
    copies = []
    for source, target in ((feat_ref, own), (adj_ref, tiles)):
        for i in range(pieces):
            some = pl.ds(i * rows, rows)
            copies.append(
                pltpu.make_async_copy(
                    source.at[t, some], target.at[some], sems.at[len(copies) // pieces, i]
                )
            )
            copies[-1].start()
    for i in range(blk_cl):
        slots[i] = (n_clus - 1) * most
    for d in range(1, n_clus):
        other = came_from(my_clus, d, n_clus)
        mask = named_mask(nbr_ref, t, first, other, blk_cl)
        for i in range(blk_cl):
            b = nbr_ref[t, nbr_k - 1, first + i] - other * blk_cl
            below = mask & (jnp.left_shift(1, b & 31) - 1)
            rank = jnp.int32(0)
            for _ in range(most):
                rank += jnp.where(below != 0, 1, 0)
                below &= below - 1
            slots[i] = jnp.where((b >= 0) & (b < blk_cl), (d - 1) * most + rank, slots[i])
    w = w_ref[...]
    for i in range(pieces):
        copies[i].wait()
        some = own[i * rows : (i + 1) * rows].reshape(rows * block, width)
        table[i * rows : (i + 1) * rows] = dot(some, w).astype(BF16).reshape(rows, block, width)
    table[blk_cl] = jnp.zeros((block, width), BF16)
    for row in range(blk_cl):
        if row % rows == 0:
            copies[pieces + row // rows].wait()
        where = [nbr_ref[t, k, first + row] - first for k in range(nbr_k)]
        where[-1] = jnp.where((where[-1] >= 0) & (where[-1] < blk_cl), where[-1], blk_cl)
        wide = jnp.concatenate([tiles[row, k] for k in range(nbr_k)], axis=1)
        acc_ref[row] = dot(wide, jnp.concatenate([table[slot] for slot in where], axis=0))


def near_sum(after, nbr, feat, adj, w, t, n_clus, most, room):
    _, blk_cl, block, width = feat.shape
    nbr_k = adj.shape[2]
    pieces = 4 if blk_cl % 4 == 0 else 1
    vmem = pl.BlockSpec(memory_space=pltpu.VMEM)
    smem = pl.BlockSpec(memory_space=pltpu.SMEM)
    hbm = pl.BlockSpec(memory_space=pltpu.HBM)
    return pl.pallas_call(
        functools.partial(near_kernel, t, n_clus, most),
        out_shape=[
            pltpu.VMEM((blk_cl, block, width), F32),
            pltpu.VMEM((blk_cl, block, width), BF16),
            pltpu.VMEM((blk_cl, nbr_k, block, block), BF16),
            jax.ShapeDtypeStruct((blk_cl,), jnp.int32),
        ],
        in_specs=[smem, smem, hbm, hbm, vmem],
        out_specs=[vmem, vmem, vmem, smem],
        scratch_shapes=[
            pltpu.VMEM((blk_cl + 1, block, width), BF16),
            pltpu.SemaphoreType.DMA((2, pieces)),
        ],
        compiler_params=pltpu.CompilerParams(vmem_limit_bytes=room << 20),
        cost_estimate=cost(NEAR_US),
        name="near_sum",
    )(after, nbr, feat, adj, w)


def far_kernel(n_snap, parts, direct, slots, acc_ref, own, tiles, w_ref, *refs):
    n_out = n_snap * len(parts)
    remote, outs = refs[: -n_out - 4], refs[-n_out - 4 : -4]
    done_ref, table, held, sems = refs[-4:]
    done_ref[0] = jnp.int32(0)
    my_snap = lax.axis_index("snap") if n_snap > 1 else jnp.int32(0)
    most, block, width = remote[0].shape
    w = w_ref[...]
    for d, ref in enumerate(remote):
        some = dot(ref[...].reshape(most * block, width), w).astype(BF16)
        table[d * most : (d + 1) * most] = some.reshape(most, block, width)
    table[len(remote) * most] = jnp.zeros((block, width), BF16)
    copies = []
    for e, (lo, hi) in enumerate(parts):
        for d in list(range(1, n_snap)) + [0]:
            p = partner(my_snap, d, n_snap)
            for g in range(lo, hi):
                row = g * n_snap + p
                total = acc_ref[row] + dot(tiles[row, tiles.shape[1] - 1], table[slots[row]])
                total = (own[row].astype(F32) + jnp.maximum(total, 0.0)).astype(BF16)
                if d == 0 or direct:
                    outs[e * n_snap + d][g - lo] = total
                else:
                    held[d - 1, g] = total
            if d > 0 and not direct:
                copies.append(
                    pltpu.make_async_copy(
                        held.at[d - 1, lo:hi], outs[e * n_snap + d], sems.at[e, d - 1]
                    )
                )
                copies[-1].start()
    for copy in copies:
        copy.wait()


def far_sum(near, remote, w, n_snap, parts, direct):
    acc, own, tiles, slots = near
    most, block, width = remote[0].shape
    vmem = pl.BlockSpec(memory_space=pltpu.VMEM)
    hbm = pl.BlockSpec(memory_space=pltpu.HBM)
    shapes = [(hi - lo, block, width) for lo, hi in parts]
    *out, done = pl.pallas_call(
        functools.partial(far_kernel, n_snap, parts, direct),
        out_shape=[
            (pltpu.VMEM if d == 0 or direct else pltpu.HBM)(shape, BF16) for shape in shapes for d in range(n_snap)
        ]
        + [jax.ShapeDtypeStruct((1,), jnp.int32)],
        in_specs=[pl.BlockSpec(memory_space=pltpu.SMEM)] + [vmem] * (4 + len(remote)),
        out_specs=[vmem if d == 0 or direct else hbm for _ in shapes for d in range(n_snap)]
        + [pl.BlockSpec(memory_space=pltpu.SMEM)],
        scratch_shapes=[
            pltpu.VMEM((len(remote) * most + 1, block, width), BF16),
            pltpu.VMEM((max(n_snap - 1, 1), parts[-1][1], block, width), BF16),
            pltpu.SemaphoreType.DMA((len(parts), max(n_snap - 1, 1))),
        ],
        compiler_params=pltpu.CompilerParams(vmem_limit_bytes=8 << 20),
        cost_estimate=cost(FAR_US),
        name="far_sum",
    )(slots, acc, own, tiles, w, *remote)
    return [out[e * n_snap : (e + 1) * n_snap] for e in range(len(parts))], done


def prepare_kernel(after_ref, pos_ref, wq_ref, wk_ref, wv_ref, wo_ref, pos, wqkv, wo, done_ref):
    done_ref[0] = jnp.int32(0)
    width = wo.shape[0]
    head_dim = width // HEADS
    to = lax.broadcasted_iota(jnp.int32, (width, width), 0)
    source = lax.broadcasted_iota(jnp.int32, (width, width), 1)
    named = (to & (HEADS - 1)) * head_dim + jnp.right_shift(to, HEADS.bit_length() - 1)
    order = jnp.where(source == named, 1.0, 0.0).astype(BF16)
    for i, ref in enumerate((wq_ref, wk_ref, wv_ref)):
        turned = lax.dot_general(
            order, ref[...], (((1,), (1,)), ((), ())), preferred_element_type=F32
        )
        wqkv[i * width : (i + 1) * width] = turned.astype(BF16)
    wo[...] = dot(order, wo_ref[...]).astype(BF16)
    pos[...] = pos_ref[...].astype(F32)


def prepare(after, pos, wq, wk, wv, wo):
    width = wo.shape[0]
    vmem = pl.BlockSpec(memory_space=pltpu.VMEM)
    return pl.pallas_call(
        prepare_kernel,
        out_shape=[
            pltpu.VMEM(pos.shape, F32),
            pltpu.VMEM((3 * width, width), BF16),
            pltpu.VMEM((width, width), BF16),
            jax.ShapeDtypeStruct((1,), jnp.int32),
        ],
        in_specs=[pl.BlockSpec(memory_space=pltpu.SMEM)] + [vmem] * 5,
        out_specs=[vmem] * 3 + [pl.BlockSpec(memory_space=pltpu.SMEM)],
        compiler_params=pltpu.CompilerParams(vmem_limit_bytes=4 << 20),
        cost_estimate=cost(1),
        name="prepare",
    )(after, pos, wq, wk, wv, wo)


def temporal_kernel(n_snap, per, blocks, chunk, *refs):
    count = n_snap * per
    ins = refs[:count]
    pos_ref, wqkv_ref, wo_ref, wup_ref, bias_ref, wdown_ref = refs[count : count + 6]
    outs = refs[-5 - n_snap : -5]
    raw, zs, qkv, att, out_sems = refs[-5:]
    me = lax.axis_index("snap")
    nsnap, nvert, width = zs.shape
    head_dim = width // HEADS
    for d in range(n_snap):
        for j in range(per):
            i = d * per + j
            raw[came_from(me, d, n_snap) * per + j] = ins[i][blocks[i]]

    for t in range(nsnap):
        zs[t] = (raw[t].astype(F32) + pos_ref[t : t + 1, :]).astype(BF16)
        qkv[t] = (
            lax.dot_general(
                wqkv_ref[...], zs[t], (((1,), (1,)), ((), ())), preferred_element_type=F32
            )
            .astype(BF16)
            .astype(F32)
        )

    def part(which, t):
        return qkv[t, which * width : (which + 1) * width, :].reshape(head_dim, HEADS, nvert)

    for t in range(nsnap):
        q = part(0, t)
        scores = [
            jnp.sum(q * part(1, s), axis=0) * (1.0 / math.sqrt(head_dim)) for s in range(t + 1)
        ]
        peak = functools.reduce(jnp.maximum, scores)
        expo = [jnp.exp(x - peak) for x in scores]
        total = functools.reduce(jnp.add, expo)
        acc = None
        for s in range(t + 1):
            prob = (expo[s] / total).astype(BF16).astype(F32)
            term = prob[None] * part(2, s)
            acc = term if acc is None else acc + term
        att[t] = acc.reshape(width, nvert).astype(BF16)

    def send(d, first):
        target = outs[d]
        if d == 0:
            target = target.at[:, pl.ds((chunk * n_snap + me) * nvert, nvert)]
        return pltpu.make_async_copy(raw.at[pl.ds(first, per)], target, out_sems.at[d])

    for g in range(n_snap):
        some = slice(g * per, (g + 1) * per)
        z = zs[some].reshape(per * nvert, width)
        joined = jnp.concatenate([att[g * per + j] for j in range(per)], axis=1)
        mixed = z.astype(F32) + lax.dot_general(
            joined, wo_ref[...], (((0,), (0,)), ((), ())), preferred_element_type=F32
        )
        hidden = jnp.maximum(dot(mixed.astype(BF16), wup_ref[...]) + bias_ref[...], 0.0)
        out = mixed + dot(hidden.astype(BF16), wdown_ref[...])
        raw[some] = out.astype(BF16).reshape(per, nvert, width)
        for d in range(n_snap):

            @pl.when(partner(me, d, n_snap) == g)
            def _():
                send(d, g * per).start()

    for d in range(n_snap):
        send(d, partner(me, d, n_snap) * per).wait()


def temporal_chunk(ins, blocks, weights, n_snap, per, chunk, chunks, result, waits):
    _, block, width = ins[0].shape
    nsnap = n_snap * per
    vmem = pl.BlockSpec(memory_space=pltpu.VMEM)
    hbm = pl.BlockSpec(memory_space=pltpu.HBM)
    before = [] if result is None else [result]
    n_in = len(ins) + len(weights)
    return pl.pallas_call(
        functools.partial(temporal_kernel, n_snap, per, blocks, chunk),
        out_shape=[pltpu.HBM((per, chunks * n_snap * block, width), BF16)]
        + [pltpu.HBM((per, block, width), BF16)] * (n_snap - 1),
        in_specs=[vmem] * (len(ins) + len(weights)) + [hbm] * len(before)
        + [pl.BlockSpec(memory_space=pltpu.SMEM)] * len(waits),
        out_specs=[hbm] * n_snap,
        input_output_aliases={n_in: 0} if before else {},
        scratch_shapes=[
            pltpu.VMEM((nsnap, block, width), BF16),
            pltpu.VMEM((nsnap, block, width), BF16),
            pltpu.VMEM((nsnap, 3 * width, block), F32),
            pltpu.VMEM((nsnap, width, block), BF16),
            pltpu.SemaphoreType.DMA((n_snap,)),
        ],
        compiler_params=pltpu.CompilerParams(vmem_limit_bytes=14 << 20),
        cost_estimate=cost(TEMPORAL_US),
        name="temporal_chunk",
    )(*ins, *weights, *before, *waits)


def place_kernel(n_snap, chunk, *refs):
    blocks, (_, out_ref, sems) = refs[: n_snap - 1], refs[n_snap - 1 :]
    block = blocks[0].shape[1]
    me = lax.axis_index("snap")
    copies = []
    for d in range(1, n_snap):
        row = (chunk * n_snap + came_from(me, d, n_snap)) * block
        copies.append(
            pltpu.make_async_copy(blocks[d - 1], out_ref.at[:, pl.ds(row, block)], sems.at[d - 1])
        )
        copies[-1].start()
    for copy in copies:
        copy.wait()


def place(result, blocks, n_snap, chunk):
    hbm = pl.BlockSpec(memory_space=pltpu.HBM)
    return pl.pallas_call(
        functools.partial(place_kernel, n_snap, chunk),
        out_shape=pltpu.HBM(result.shape, result.dtype),
        in_specs=[pl.BlockSpec(memory_space=pltpu.VMEM)] * len(blocks) + [hbm],
        out_specs=hbm,
        input_output_aliases={len(blocks): 0},
        scratch_shapes=[pltpu.SemaphoreType.DMA((n_snap - 1,))],
        compiler_params=pltpu.CompilerParams(vmem_limit_bytes=1 << 20),
        cost_estimate=cost(PLACE_US),
        name="place",
    )(*blocks, result)


def shift(x, d, n):
    return lax.ppermute(x, "snap", [(i, partner(i, d, n)) for i in range(n)])


def temporal_fast(got, parts, weights, n_snap, first):
    per = len(got)
    chunks = parts[0][-1][1]
    result, backs = None, []
    for c in range(chunks):
        ins, blocks = [], []
        for d in range(n_snap):
            for j in range(per):
                e = [lo <= c < hi for lo, hi in parts[j]].index(True)
                ins.append(got[j][e][d])
                blocks.append(c - parts[j][e][0])
        result, *sent = temporal_chunk(
            ins, blocks, weights, n_snap, per, c, chunks, result, first if c == 0 else []
        )
        backs.append([shift(x, d + 1, n_snap) for d, x in enumerate(sent)])
        if c >= LAG:
            result = place(result, backs[c - LAG], n_snap, c - LAG)
    for c in range(max(chunks - LAG, 0), chunks):
        result = place(result, backs[c], n_snap, c)
    return result


def temporal_plain(zvals, w_query, w_key, w_value, w_out, w_up, up_bias, w_down):
    nsnap, nvert, width = zvals.shape
    head_dim = width // HEADS
    heads = (nsnap, nvert, HEADS, head_dim)
    q_heads = dot(zvals, w_query).astype(BF16).reshape(heads)
    k_heads = dot(zvals, w_key).astype(BF16).reshape(heads)
    v_heads = dot(zvals, w_value).astype(BF16).reshape(heads)
    scores = jnp.einsum("tvhd,svhd->vhts", q_heads, k_heads, preferred_element_type=F32)
    scores = scores * (1.0 / math.sqrt(head_dim))
    causal = jnp.arange(nsnap)[:, None] >= jnp.arange(nsnap)[None, :]
    scores = jnp.where(causal, scores, NEG)
    peak = jnp.max(scores, axis=-1, keepdims=True)
    expo = jnp.exp(scores - peak)
    probs = (expo / jnp.sum(expo, axis=-1, keepdims=True)).astype(BF16)
    attended = jnp.einsum("vhts,svhd->tvhd", probs, v_heads, preferred_element_type=F32)
    attended = attended.astype(BF16).reshape(nsnap, nvert, width)
    mixed = zvals.astype(F32) + dot(attended, w_out)
    hidden = jax.nn.relu(dot(mixed.astype(BF16), w_up) + up_bias).astype(BF16)
    return (mixed + dot(hidden, w_down)).astype(BF16)


def on_device(
    features,
    adj_tiles,
    neighbors,
    w_struct,
    pos_embed,
    w_query,
    w_key,
    w_value,
    w_out,
    w_up,
    up_bias,
    w_down,
):
    snap_dev, vert_cl, width = features.shape
    blk_cl, nbr_k, block = adj_tiles.shape[1:4]
    n_clus, n_snap = lax.axis_size("clus"), lax.axis_size("snap")
    most = 4
    nbr = neighbors.transpose(0, 2, 1)
    feat = features.reshape(snap_dev, blk_cl, block, width)
    fast = snap_dev * n_snap <= 8 and blk_cl % n_snap == 0 and block % LANES == 0
    groups = n_snap if fast else 1
    chunks = blk_cl // groups
    done = jnp.zeros((1,), jnp.int32)
    sets = []
    for t in range(snap_dev):
        some, done = gather_blocks(done, nbr, feat, t, most, n_clus)
        sets.append(some)
    got, parts = [], []
    for t in range(snap_dev):
        near = near_sum(done, nbr, feat, adj_tiles, w_struct, t, n_clus, most, ROOM[min(t, 1)])
        if t == 0:
            for later in range(1, snap_dev):
                sets[later], _ = gate(near[:1], sets[later])
        remote = {}
        for d in range(n_clus - 1, 0, -1):
            pairs = [(i, partner(i, d, n_clus)) for i in range(n_clus)]
            remote[d] = lax.ppermute(sets[t][d - 1], "clus", pairs)
        remote = [remote[d] for d in range(1, n_clus)]
        last = t == snap_dev - 1 and fast and chunks > 1
        parts.append([(0, 1), (1, chunks)] if last else [(0, chunks)])
        sent, done = far_sum(near, remote, w_struct, groups, parts[-1], t == 0)
        if t == 0 and fast:
            *prepared, done = prepare(done, pos_embed, w_query, w_key, w_value, w_out)
        got.append([])
        for e, part in enumerate(sent):
            if t > 0 and n_snap > 2:
                waits = got[-2][-1][1:2] if e == 0 else got[-1][-1][1:2]
                part[1:], done = gate(waits, part[1:])
            got[-1].append([x if d == 0 else shift(x, d, n_snap) for d, x in enumerate(part)])
    if fast:
        weights = (*prepared, w_up, up_bias.reshape(1, -1), w_down)
        return temporal_fast(got, parts, weights, n_snap, [done])
    vert_dev = vert_cl // n_snap
    struct_out = jnp.stack([g[0][0].reshape(n_snap, vert_dev, width) for g in got])
    inputs = lax.all_to_all(struct_out, "snap", split_axis=1, concat_axis=0, tiled=True)[:, 0]
    zvals = (inputs.astype(F32) + pos_embed.astype(F32)[:, None, :]).astype(BF16)
    result = temporal_plain(zvals, w_query, w_key, w_value, w_out, w_up, up_bias, w_down)
    returned = lax.all_to_all(
        result[:, None], "snap", split_axis=0, concat_axis=1, tiled=True
    )
    return returned.reshape(snap_dev, vert_cl, width)


def solution(mesh):
    placed = (
        P(("grp", "snap"), "clus", None),
        P(("grp", "snap"), "clus", None, None, None),
        P(("grp", "snap"), None, None),
        P(),
        P(),
        P(),
        P(),
        P(),
        P(),
        P(),
        P(),
        P(),
    )
    return jax.shard_map(
        on_device,
        mesh=mesh,
        in_specs=placed,
        out_specs=P(("grp", "snap"), "clus", None),
        check_vma=False,
    )
```

```python
import functools
import math

import jax
import jax.numpy as jnp
from jax import lax
from jax.experimental import pallas as pl
from jax.experimental.pallas import tpu as pltpu
from jax.sharding import PartitionSpec as P

HEADS = 8
LANES = 128
LAG = 3
ALONE, ROOM = 60, (57, 46)
GATHER_US, GATE_US, NEAR_US, FAR_US, TEMPORAL_US, PLACE_US = 3, 0.5, 3, 2, 3, 1
NEG = -1e30
F32 = jnp.float32
BF16 = jnp.bfloat16


def cost(us):
    return pl.CostEstimate(flops=0, bytes_accessed=int(us * 3.0e4), transcendentals=0)


def dot(a, b):
    return jnp.dot(a, b, preferred_element_type=F32)


def partner(me, d, n):
    return me ^ d if n & (n - 1) == 0 else (me + d) % n


def came_from(me, d, n):
    return me ^ d if n & (n - 1) == 0 else (me + n - d) % n


def named_mask(nbr_ref, t, first, cluster, blk_cl):
    last = nbr_ref.shape[1] - 1
    base = cluster * blk_cl
    mask = jnp.int32(0)
    for i in range(blk_cl):
        g = nbr_ref[t, last, first + i] - base
        mask |= jnp.where((g >= 0) & (g < blk_cl), jnp.left_shift(1, g & 31), 0)
    return mask


def lowest_bit(mask, blk_cl):
    low = mask & -mask
    place = jnp.int32(0)
    for i in range((blk_cl - 1).bit_length()):
        holes = sum(1 << b for b in range(blk_cl) if b >> i & 1)
        place += jnp.where((low & holes) != 0, 1 << i, 0)
    return place


def gather_kernel(t, most, n_clus, direct, after_ref, nbr_ref, feat_ref, *refs):
    blk_cl = feat_ref.shape[1]
    outs, (done_ref, held, in_sems, out_sems) = refs[: n_clus - 1], refs[n_clus - 1 :]
    done_ref[0] = jnp.int32(0)
    me = lax.axis_index("clus")
    arrivals, copies = {}, []
    order = list(range(n_clus - 1, 0, -1))
    for d in order:
        mask = named_mask(nbr_ref, t, partner(me, d, n_clus) * blk_cl, me, blk_cl)
        picked = []
        for _ in range(most):
            picked.append(lowest_bit(mask, blk_cl))
            mask &= mask - 1
        target = outs[d - 1] if direct else held.at[d - 1]
        arrivals[d] = [
            pltpu.make_async_copy(feat_ref.at[t, picked[j]], target.at[j], in_sems.at[d - 1, j])
            for j in range(most)
        ]
        for copy in arrivals[d]:
            copy.start()
    for d in order:
        for copy in arrivals[d]:
            copy.wait()
        if not direct:
            copies.append(pltpu.make_async_copy(held.at[d - 1], outs[d - 1], out_sems.at[d - 1]))
            copies[-1].start()
    for copy in copies:
        copy.wait()


def gather_blocks(after, nbr, feat, t, most, n_clus):
    direct = t == 0
    _, _, block, width = feat.shape
    shape = (most, block, width)
    smem = pl.BlockSpec(memory_space=pltpu.SMEM)
    space = pltpu.VMEM if direct else pltpu.HBM
    *out, done = pl.pallas_call(
        functools.partial(gather_kernel, t, most, n_clus, direct),
        out_shape=[space(shape, BF16)] * (n_clus - 1) + [jax.ShapeDtypeStruct((1,), jnp.int32)],
        in_specs=[pl.BlockSpec(memory_space=pl.ANY), smem, pl.BlockSpec(memory_space=pltpu.HBM)],
        out_specs=[pl.BlockSpec(memory_space=space)] * (n_clus - 1) + [smem],
        scratch_shapes=[
            pltpu.VMEM((n_clus - 1,) + (shape if not direct else (1, 16, 128)), BF16),
            pltpu.SemaphoreType.DMA((n_clus - 1, most)),
            pltpu.SemaphoreType.DMA((n_clus - 1,)),
        ],
        compiler_params=pltpu.CompilerParams(vmem_limit_bytes=ALONE << 20),
        cost_estimate=cost(GATHER_US),
        name="gather_blocks",
    )(after, nbr, feat)
    return out, done


def gate_kernel(*refs):
    refs[-1][0] = jnp.int32(0)


def gate(after, xs):
    hbm = pl.BlockSpec(memory_space=pltpu.HBM)
    *out, done = pl.pallas_call(
        gate_kernel,
        out_shape=[pltpu.HBM(x.shape, x.dtype) for x in xs]
        + [jax.ShapeDtypeStruct((1,), jnp.int32)],
        in_specs=[pl.BlockSpec(memory_space=pl.ANY)] * len(after) + [hbm] * len(xs),
        out_specs=[hbm] * len(xs) + [pl.BlockSpec(memory_space=pltpu.SMEM)],
        input_output_aliases={i + len(after): i for i in range(len(xs))},
        compiler_params=pltpu.CompilerParams(vmem_limit_bytes=1 << 20),
        cost_estimate=cost(GATE_US),
        name="gate",
    )(*after, *xs)
    return out, done


def near_kernel(
    t, n_clus, most, after_ref, nbr_ref, feat_ref, adj_ref, w_ref, acc_ref, own, tiles, slots, table, sems
):
    my_clus = lax.axis_index("clus")
    blk_cl, block, width = own.shape
    nbr_k = tiles.shape[1]
    pieces = sems.shape[1]
    rows = blk_cl // pieces
    first = my_clus * blk_cl
    copies = []
    for source, target in ((feat_ref, own), (adj_ref, tiles)):
        for i in range(pieces):
            some = pl.ds(i * rows, rows)
            copies.append(
                pltpu.make_async_copy(
                    source.at[t, some], target.at[some], sems.at[len(copies) // pieces, i]
                )
            )
            copies[-1].start()
    for i in range(blk_cl):
        slots[i] = (n_clus - 1) * most
    for d in range(1, n_clus):
        other = came_from(my_clus, d, n_clus)
        mask = named_mask(nbr_ref, t, first, other, blk_cl)
        for i in range(blk_cl):
            b = nbr_ref[t, nbr_k - 1, first + i] - other * blk_cl
            below = mask & (jnp.left_shift(1, b & 31) - 1)
            rank = jnp.int32(0)
            for _ in range(most):
                rank += jnp.where(below != 0, 1, 0)
                below &= below - 1
            slots[i] = jnp.where((b >= 0) & (b < blk_cl), (d - 1) * most + rank, slots[i])
    w = w_ref[...]
    for i in range(pieces):
        copies[i].wait()
        some = own[i * rows : (i + 1) * rows].reshape(rows * block, width)
        table[i * rows : (i + 1) * rows] = dot(some, w).astype(BF16).reshape(rows, block, width)
    table[blk_cl] = jnp.zeros((block, width), BF16)
    for row in range(blk_cl):
        if row % rows == 0:
            copies[pieces + row // rows].wait()
        where = [nbr_ref[t, k, first + row] - first for k in range(nbr_k)]
        where[-1] = jnp.where((where[-1] >= 0) & (where[-1] < blk_cl), where[-1], blk_cl)
        wide = jnp.concatenate([tiles[row, k] for k in range(nbr_k)], axis=1)
        acc_ref[row] = dot(wide, jnp.concatenate([table[slot] for slot in where], axis=0))


def near_sum(after, nbr, feat, adj, w, t, n_clus, most, room):
    _, blk_cl, block, width = feat.shape
    nbr_k = adj.shape[2]
    pieces = 4 if blk_cl % 4 == 0 else 1
    vmem = pl.BlockSpec(memory_space=pltpu.VMEM)
    smem = pl.BlockSpec(memory_space=pltpu.SMEM)
    hbm = pl.BlockSpec(memory_space=pltpu.HBM)
    return pl.pallas_call(
        functools.partial(near_kernel, t, n_clus, most),
        out_shape=[
            pltpu.VMEM((blk_cl, block, width), F32),
            pltpu.VMEM((blk_cl, block, width), BF16),
            pltpu.VMEM((blk_cl, nbr_k, block, block), BF16),
            jax.ShapeDtypeStruct((blk_cl,), jnp.int32),
        ],
        in_specs=[pl.BlockSpec(memory_space=pl.ANY), smem, hbm, hbm, vmem],
        out_specs=[vmem, vmem, vmem, smem],
        scratch_shapes=[
            pltpu.VMEM((blk_cl + 1, block, width), BF16),
            pltpu.SemaphoreType.DMA((2, pieces)),
        ],
        compiler_params=pltpu.CompilerParams(vmem_limit_bytes=room << 20),
        cost_estimate=cost(NEAR_US),
        name="near_sum",
    )(after, nbr, feat, adj, w)


def far_kernel(n_snap, parts, direct, slots, acc_ref, own, tiles, w_ref, *refs):
    n_out = n_snap * len(parts)
    remote, outs = refs[: -n_out - 4], refs[-n_out - 4 : -4]
    done_ref, table, held, sems = refs[-4:]
    done_ref[0] = jnp.int32(0)
    my_snap = lax.axis_index("snap") if n_snap > 1 else jnp.int32(0)
    most, block, width = remote[0].shape
    w = w_ref[...]
    for d, ref in enumerate(remote):
        some = dot(ref[...].reshape(most * block, width), w).astype(BF16)
        table[d * most : (d + 1) * most] = some.reshape(most, block, width)
    table[len(remote) * most] = jnp.zeros((block, width), BF16)
    copies = []
    for e, (lo, hi) in enumerate(parts):
        for d in list(range(1, n_snap)) + [0]:
            p = partner(my_snap, d, n_snap)
            for g in range(lo, hi):
                row = g * n_snap + p
                total = acc_ref[row] + dot(tiles[row, tiles.shape[1] - 1], table[slots[row]])
                total = (own[row].astype(F32) + jnp.maximum(total, 0.0)).astype(BF16)
                if d == 0 or direct:
                    outs[e * n_snap + d][g - lo] = total
                else:
                    held[d - 1, g] = total
            if d > 0 and not direct:
                copies.append(
                    pltpu.make_async_copy(
                        held.at[d - 1, lo:hi], outs[e * n_snap + d], sems.at[e, d - 1]
                    )
                )
                copies[-1].start()
    for copy in copies:
        copy.wait()


def far_sum(near, remote, w, n_snap, parts, direct):
    acc, own, tiles, slots = near
    most, block, width = remote[0].shape
    vmem = pl.BlockSpec(memory_space=pltpu.VMEM)
    hbm = pl.BlockSpec(memory_space=pltpu.HBM)
    shapes = [(hi - lo, block, width) for lo, hi in parts]
    *out, done = pl.pallas_call(
        functools.partial(far_kernel, n_snap, parts, direct),
        out_shape=[
            (pltpu.VMEM if d == 0 or direct else pltpu.HBM)(shape, BF16) for shape in shapes for d in range(n_snap)
        ]
        + [jax.ShapeDtypeStruct((1,), jnp.int32)],
        in_specs=[pl.BlockSpec(memory_space=pltpu.SMEM)] + [vmem] * (4 + len(remote)),
        out_specs=[vmem if d == 0 or direct else hbm for _ in shapes for d in range(n_snap)]
        + [pl.BlockSpec(memory_space=pltpu.SMEM)],
        scratch_shapes=[
            pltpu.VMEM((len(remote) * most + 1, block, width), BF16),
            pltpu.VMEM((max(n_snap - 1, 1), parts[-1][1], block, width), BF16),
            pltpu.SemaphoreType.DMA((len(parts), max(n_snap - 1, 1))),
        ],
        compiler_params=pltpu.CompilerParams(vmem_limit_bytes=8 << 20),
        cost_estimate=cost(FAR_US),
        name="far_sum",
    )(slots, acc, own, tiles, w, *remote)
    return [out[e * n_snap : (e + 1) * n_snap] for e in range(len(parts))], done


def prepare_kernel(after_ref, pos_ref, wq_ref, wk_ref, wv_ref, wo_ref, pos, wqkv, wo, done_ref):
    done_ref[0] = jnp.int32(0)
    width = wo.shape[0]
    head_dim = width // HEADS
    to = lax.broadcasted_iota(jnp.int32, (width, width), 0)
    source = lax.broadcasted_iota(jnp.int32, (width, width), 1)
    named = (to & (HEADS - 1)) * head_dim + jnp.right_shift(to, HEADS.bit_length() - 1)
    order = jnp.where(source == named, 1.0, 0.0).astype(BF16)
    for i, ref in enumerate((wq_ref, wk_ref, wv_ref)):
        turned = lax.dot_general(
            order, ref[...], (((1,), (1,)), ((), ())), preferred_element_type=F32
        )
        wqkv[i * width : (i + 1) * width] = turned.astype(BF16)
    wo[...] = dot(order, wo_ref[...]).astype(BF16)
    pos[...] = pos_ref[...].astype(F32)


def prepare(after, pos, wq, wk, wv, wo):
    width = wo.shape[0]
    vmem = pl.BlockSpec(memory_space=pltpu.VMEM)
    return pl.pallas_call(
        prepare_kernel,
        out_shape=[
            pltpu.VMEM(pos.shape, F32),
            pltpu.VMEM((3 * width, width), BF16),
            pltpu.VMEM((width, width), BF16),
            jax.ShapeDtypeStruct((1,), jnp.int32),
        ],
        in_specs=[pl.BlockSpec(memory_space=pl.ANY)] + [vmem] * 5,
        out_specs=[vmem] * 3 + [pl.BlockSpec(memory_space=pltpu.SMEM)],
        compiler_params=pltpu.CompilerParams(vmem_limit_bytes=4 << 20),
        cost_estimate=cost(1),
        name="prepare",
    )(after, pos, wq, wk, wv, wo)


def temporal_kernel(n_snap, per, blocks, chunk, *refs):
    count = n_snap * per
    ins = refs[:count]
    pos_ref, wqkv_ref, wo_ref, wup_ref, bias_ref, wdown_ref = refs[count : count + 6]
    outs = refs[-5 - n_snap : -5]
    raw, zs, qkv, att, out_sems = refs[-5:]
    me = lax.axis_index("snap")
    nsnap, nvert, width = zs.shape
    head_dim = width // HEADS
    for d in range(n_snap):
        for j in range(per):
            i = d * per + j
            raw[came_from(me, d, n_snap) * per + j] = ins[i][blocks[i]]

    for t in range(nsnap):
        zs[t] = (raw[t].astype(F32) + pos_ref[t : t + 1, :]).astype(BF16)
        qkv[t] = (
            lax.dot_general(
                wqkv_ref[...], zs[t], (((1,), (1,)), ((), ())), preferred_element_type=F32
            )
            .astype(BF16)
            .astype(F32)
        )

    def part(which, t):
        return qkv[t, which * width : (which + 1) * width, :].reshape(head_dim, HEADS, nvert)

    for t in range(nsnap):
        q = part(0, t)
        scores = [
            jnp.sum(q * part(1, s), axis=0) * (1.0 / math.sqrt(head_dim)) for s in range(t + 1)
        ]
        peak = functools.reduce(jnp.maximum, scores)
        expo = [jnp.exp(x - peak) for x in scores]
        total = functools.reduce(jnp.add, expo)
        acc = None
        for s in range(t + 1):
            prob = (expo[s] / total).astype(BF16).astype(F32)
            term = prob[None] * part(2, s)
            acc = term if acc is None else acc + term
        att[t] = acc.reshape(width, nvert).astype(BF16)

    def send(d, first):
        target = outs[d]
        if d == 0:
            target = target.at[:, pl.ds((chunk * n_snap + me) * nvert, nvert)]
        return pltpu.make_async_copy(raw.at[pl.ds(first, per)], target, out_sems.at[d])

    for g in range(n_snap):
        some = slice(g * per, (g + 1) * per)
        z = zs[some].reshape(per * nvert, width)
        joined = jnp.concatenate([att[g * per + j] for j in range(per)], axis=1)
        mixed = z.astype(F32) + lax.dot_general(
            joined, wo_ref[...], (((0,), (0,)), ((), ())), preferred_element_type=F32
        )
        hidden = jnp.maximum(dot(mixed.astype(BF16), wup_ref[...]) + bias_ref[...], 0.0)
        out = mixed + dot(hidden.astype(BF16), wdown_ref[...])
        raw[some] = out.astype(BF16).reshape(per, nvert, width)
        for d in range(n_snap):

            @pl.when(partner(me, d, n_snap) == g)
            def _():
                send(d, g * per).start()

    for d in range(n_snap):
        send(d, partner(me, d, n_snap) * per).wait()


def temporal_chunk(ins, blocks, weights, n_snap, per, chunk, chunks, result, waits):
    _, block, width = ins[0].shape
    nsnap = n_snap * per
    vmem = pl.BlockSpec(memory_space=pltpu.VMEM)
    hbm = pl.BlockSpec(memory_space=pltpu.HBM)
    before = [] if result is None else [result]
    n_in = len(ins) + len(weights)
    return pl.pallas_call(
        functools.partial(temporal_kernel, n_snap, per, blocks, chunk),
        out_shape=[pltpu.HBM((per, chunks * n_snap * block, width), BF16)]
        + [pltpu.HBM((per, block, width), BF16)] * (n_snap - 1),
        in_specs=[vmem] * (len(ins) + len(weights)) + [hbm] * len(before)
        + [pl.BlockSpec(memory_space=pltpu.SMEM)] * len(waits),
        out_specs=[hbm] * n_snap,
        input_output_aliases={n_in: 0} if before else {},
        scratch_shapes=[
            pltpu.VMEM((nsnap, block, width), BF16),
            pltpu.VMEM((nsnap, block, width), BF16),
            pltpu.VMEM((nsnap, 3 * width, block), F32),
            pltpu.VMEM((nsnap, width, block), BF16),
            pltpu.SemaphoreType.DMA((n_snap,)),
        ],
        compiler_params=pltpu.CompilerParams(vmem_limit_bytes=14 << 20),
        cost_estimate=cost(TEMPORAL_US),
        name="temporal_chunk",
    )(*ins, *weights, *before, *waits)


def place_kernel(n_snap, chunk, *refs):
    blocks, (_, out_ref, sems) = refs[: n_snap - 1], refs[n_snap - 1 :]
    block = blocks[0].shape[1]
    me = lax.axis_index("snap")
    copies = []
    for d in range(1, n_snap):
        row = (chunk * n_snap + came_from(me, d, n_snap)) * block
        copies.append(
            pltpu.make_async_copy(blocks[d - 1], out_ref.at[:, pl.ds(row, block)], sems.at[d - 1])
        )
        copies[-1].start()
    for copy in copies:
        copy.wait()


def place(result, blocks, n_snap, chunk):
    hbm = pl.BlockSpec(memory_space=pltpu.HBM)
    return pl.pallas_call(
        functools.partial(place_kernel, n_snap, chunk),
        out_shape=pltpu.HBM(result.shape, result.dtype),
        in_specs=[pl.BlockSpec(memory_space=pltpu.VMEM)] * len(blocks) + [hbm],
        out_specs=hbm,
        input_output_aliases={len(blocks): 0},
        scratch_shapes=[pltpu.SemaphoreType.DMA((n_snap - 1,))],
        compiler_params=pltpu.CompilerParams(vmem_limit_bytes=1 << 20),
        cost_estimate=cost(PLACE_US),
        name="place",
    )(*blocks, result)


def shift(x, d, n):
    return lax.ppermute(x, "snap", [(i, partner(i, d, n)) for i in range(n)])


def temporal_fast(got, parts, weights, n_snap, first):
    per = len(got)
    chunks = parts[0][-1][1]
    result, backs = None, []
    for c in range(chunks):
        ins, blocks = [], []
        for d in range(n_snap):
            for j in range(per):
                e = [lo <= c < hi for lo, hi in parts[j]].index(True)
                ins.append(got[j][e][d])
                blocks.append(c - parts[j][e][0])
        result, *sent = temporal_chunk(
            ins, blocks, weights, n_snap, per, c, chunks, result, first if c == 0 else []
        )
        backs.append([shift(x, d + 1, n_snap) for d, x in enumerate(sent)])
        if c >= LAG:
            result = place(result, backs[c - LAG], n_snap, c - LAG)
    for c in range(max(chunks - LAG, 0), chunks):
        result = place(result, backs[c], n_snap, c)
    return result


def temporal_plain(zvals, w_query, w_key, w_value, w_out, w_up, up_bias, w_down):
    nsnap, nvert, width = zvals.shape
    head_dim = width // HEADS
    heads = (nsnap, nvert, HEADS, head_dim)
    q_heads = dot(zvals, w_query).astype(BF16).reshape(heads)
    k_heads = dot(zvals, w_key).astype(BF16).reshape(heads)
    v_heads = dot(zvals, w_value).astype(BF16).reshape(heads)
    scores = jnp.einsum("tvhd,svhd->vhts", q_heads, k_heads, preferred_element_type=F32)
    scores = scores * (1.0 / math.sqrt(head_dim))
    causal = jnp.arange(nsnap)[:, None] >= jnp.arange(nsnap)[None, :]
    scores = jnp.where(causal, scores, NEG)
    peak = jnp.max(scores, axis=-1, keepdims=True)
    expo = jnp.exp(scores - peak)
    probs = (expo / jnp.sum(expo, axis=-1, keepdims=True)).astype(BF16)
    attended = jnp.einsum("vhts,svhd->tvhd", probs, v_heads, preferred_element_type=F32)
    attended = attended.astype(BF16).reshape(nsnap, nvert, width)
    mixed = zvals.astype(F32) + dot(attended, w_out)
    hidden = jax.nn.relu(dot(mixed.astype(BF16), w_up) + up_bias).astype(BF16)
    return (mixed + dot(hidden, w_down)).astype(BF16)


def on_device(
    features,
    adj_tiles,
    neighbors,
    w_struct,
    pos_embed,
    w_query,
    w_key,
    w_value,
    w_out,
    w_up,
    up_bias,
    w_down,
):
    snap_dev, vert_cl, width = features.shape
    blk_cl, nbr_k, block = adj_tiles.shape[1:4]
    n_clus, n_snap = lax.axis_size("clus"), lax.axis_size("snap")
    most = 4
    nbr = neighbors.transpose(0, 2, 1)
    feat = features.reshape(snap_dev, blk_cl, block, width)
    fast = snap_dev * n_snap <= 8 and blk_cl % n_snap == 0 and block % LANES == 0
    groups = n_snap if fast else 1
    chunks = blk_cl // groups
    done = jnp.zeros((1,), jnp.int32)
    sets = []
    for t in range(snap_dev):
        some, done = gather_blocks(done, nbr, feat, t, most, n_clus)
        sets.append(some)
    got, parts = [], []
    for t in range(snap_dev):
        near = near_sum(done, nbr, feat, adj_tiles, w_struct, t, n_clus, most, ROOM[min(t, 1)])
        if t == 0:
            for later in range(1, snap_dev):
                sets[later], _ = gate(near[:1], sets[later])
        remote = {}
        for d in range(n_clus - 1, 0, -1):
            pairs = [(i, partner(i, d, n_clus)) for i in range(n_clus)]
            remote[d] = lax.ppermute(sets[t][d - 1], "clus", pairs)
        remote = [remote[d] for d in range(1, n_clus)]
        last = t == snap_dev - 1 and fast and chunks > 1
        parts.append([(0, 1), (1, chunks)] if last else [(0, chunks)])
        sent, done = far_sum(near, remote, w_struct, groups, parts[-1], t == 0)
        if t == 0 and fast:
            *prepared, done = prepare(done, pos_embed, w_query, w_key, w_value, w_out)
        got.append([])
        for e, part in enumerate(sent):
            if t > 0 and n_snap > 2:
                waits = got[-2][-1][1:2] if e == 0 else got[-1][-1][1:2]
                part[1:], done = gate(waits, part[1:])
            got[-1].append([x if d == 0 else shift(x, d, n_snap) for d, x in enumerate(part)])
    if fast:
        weights = (*prepared, w_up, up_bias.reshape(1, -1), w_down)
        return temporal_fast(got, parts, weights, n_snap, [done])
    vert_dev = vert_cl // n_snap
    struct_out = jnp.stack([g[0][0].reshape(n_snap, vert_dev, width) for g in got])
    inputs = lax.all_to_all(struct_out, "snap", split_axis=1, concat_axis=0, tiled=True)[:, 0]
    zvals = (inputs.astype(F32) + pos_embed.astype(F32)[:, None, :]).astype(BF16)
    result = temporal_plain(zvals, w_query, w_key, w_value, w_out, w_up, up_bias, w_down)
    returned = lax.all_to_all(
        result[:, None], "snap", split_axis=0, concat_axis=1, tiled=True
    )
    return returned.reshape(snap_dev, vert_cl, width)


def solution(mesh):
    placed = (
        P(("grp", "snap"), "clus", None),
        P(("grp", "snap"), "clus", None, None, None),
        P(("grp", "snap"), None, None),
        P(),
        P(),
        P(),
        P(),
        P(),
        P(),
        P(),
        P(),
        P(),
    )
    return jax.shard_map(
        on_device,
        mesh=mesh,
        in_specs=placed,
        out_specs=P(("grp", "snap"), "clus", None),
        check_vma=False,
    )
```
